256 devices in a mesh: chan: 32 (over z, x), slab: 2 (over core), batch: 4 (over y).
Axes of the slice: x: 4, y: 4, z: 8, core: 2. Of those that a mesh axis runs over, the one named last changes fastest.
Arguments:
- inputs: bfloat16 [2048, 8, 512], P(('batch', 'chan'), 'slab'), parts along dimension 0, may hold values from -6 to 6
- weights: bfloat16 [27, 512, 512], P(None, 'chan'), may hold values from -0.09375 to 0.09375
- out_grad: bfloat16 [2048, 8, 512], P(('batch', 'chan'), 'slab'), parts along dimension 0, may hold values from -6 to 6
Outputs:
- conv_out: bfloat16 [2048, 8, 512], P(('batch', 'chan'), 'slab'), parts along dimension 0
- input_grad: bfloat16 [2048, 8, 512], P(('batch', 'chan'), 'slab'), parts along dimension 0
The draws below stay inside these ranges and needn't reach their ends.
There are 4 independent parts, one for each index of `batch`. The reference program is written for one: setup_inputs(seed, part) draws one part's arguments, and reference() takes and returns one part's arrays. A program takes and returns all parts, laid end to end along the dimension named above; an argument that names none is the same for every part. Nothing has to cross between parts.
All inputs are finite; a program needn't handle non-finite values.
Results may differ from the reference program's by a relative error of at most 0.0013.
Values may be sent and summed in bfloat16 or wider, within the bound.
A program may use at most 192 MiB of HBM per device.

```python
import jax
import jax.numpy as jnp
from jax import lax

CIN = 512
COUT = 512
NY = 8
NZ = 64
NX = 8


def with_spikes(result, key, source, target, shards_of, factor):
    owner, partner = [(jnp.arange(result.shape[dim]) // (result.shape[dim] // shards_of)).reshape([-1 if axis == dim else 1 for axis in range(result.ndim)]) for dim in (source, target)]
    chosen = jax.random.permutation(key, shards_of)[partner]
    strong = (owner == chosen) | (owner == (partner + shards_of // 2) % shards_of)
    return jnp.where(strong, factor * result, result)


def shard_levels(stream_key, extent, cuts, smallest, top_value):
    gain, own = 1.0, jax.random.fold_in(stream_key, 6)
    for axis_at, blocks in cuts:
        heights = jnp.exp(jax.random.uniform(jax.random.fold_in(own, axis_at), (blocks,), jnp.float32, smallest / len(cuts), top_value / len(cuts)))
        gain = gain * jnp.repeat(heights, extent[axis_at] // blocks).reshape([-1 if axis == axis_at else 1 for axis in range(len(extent))])
    return gain


def scatter_about(stream_key, shape, spread, most, shards=(), kind=jnp.bfloat16):
    result = jax.random.normal(stream_key, shape, jnp.float32) * spread
    if len(shards) > 0:
        result = shard_levels(stream_key, shape, shards, -0.22, 0.18) * result
    return jnp.clip(result, min=-most, max=most).astype(kind)


def bell_draw_with(rng, shape, scale, bound, shards, heavy, dtype=jnp.bfloat16):
    values = scale * jax.random.normal(rng, shape, jnp.float32)
    if shards:
        values = values * shard_levels(rng, shape, shards, -0.22, 0.18)
    return jnp.clip(with_spikes(values, jax.random.fold_in(rng, 3), *heavy), -bound, bound).astype(dtype)


def setup_inputs(seed: int = 0, part: int = 0) -> dict:
    splits = jax.random.split(jax.random.key(seed), 4)
    part_keys = jax.random.split(jax.random.fold_in(splits[3], part), 4)
    inputs = scatter_about(part_keys[0], (CIN, NX, NY * NZ), 1.0, 6.0, ((0, 32), (1, 2)))
    weights = bell_draw_with(splits[1], (27, CIN, COUT), (27 * CIN) ** -0.5, 0.09375, ((1, 32),), (1, 2, 32, 2.75))
    out_grad = scatter_about(part_keys[2], (COUT, NX, NY * NZ), 1.0, 6.0, ((0, 32), (1, 2)))
    return dict(inputs=inputs, weights=weights, out_grad=out_grad)


OFFSETS = (-1, 0, 1)


def reference(inputs, weights, out_grad):
    field_in = inputs.astype(jnp.float32).reshape(CIN, NX, NY, NZ)
    field_grad = out_grad.astype(jnp.float32).reshape(COUT, NX, NY, NZ)
    kernel = weights.astype(jnp.float32)
    forward = jnp.zeros((COUT, NX, NY, NZ), jnp.float32)
    backward = jnp.zeros((CIN, NX, NY, NZ), jnp.float32)
    for offset_x in OFFSETS:
        for offset_y in OFFSETS:
            for offset_z in OFFSETS:
                number = 9 * (offset_x + 1) + 3 * (offset_y + 1) + (offset_z + 1)
                moved_in = jnp.roll(field_in, (-offset_x, -offset_y, -offset_z), axis=(1, 2, 3))
                forward = forward + jnp.einsum("io,ixyz->oxyz", kernel[number], moved_in, precision=lax.Precision.HIGHEST)
                moved_grad = jnp.roll(field_grad, (offset_x, offset_y, offset_z), axis=(1, 2, 3))
                backward = backward + jnp.einsum("io,oxyz->ixyz", kernel[number], moved_grad, precision=lax.Precision.HIGHEST)
    conv_out = forward.reshape(COUT, NX, NY * NZ).astype(jnp.bfloat16)
    input_grad = backward.reshape(CIN, NX, NY * NZ).astype(jnp.bfloat16)
    return (conv_out, input_grad)
```

```python
import jax
import jax.numpy as jnp
from jax import lax
from jax.experimental import pallas as pl
from jax.experimental.pallas import tpu as pltpu
from jax.sharding import PartitionSpec as P

BF = jnp.bfloat16
F32 = jnp.float32
MESH = pl.DeviceIdType.MESH
NXC = 4
NZC = 8


def remote(src, dst, send, recv, chan, slab):
    return pltpu.make_async_remote_copy(
        src_ref=src,
        dst_ref=dst,
        send_sem=send,
        recv_sem=recv,
        device_id={"chan": chan, "slab": slab},
        device_id_type=MESH,
    )


def arrived(ref, sem):
    pltpu.make_async_copy(ref, ref, sem).wait()


def iota(shape, dim):
    return lax.broadcasted_iota(jnp.int32, shape, dim)


def kernel(
    g_ref, x_ref, w_ref, go_ref, co_ref,
    perm, permw, part, acts, wl, wpack, wrecv, wfwd, wbwd, outs, outr, hprod,
    loc_sem, xs, xr, zs, zr, ss, sr, ws, wr, fs, fr, bs, br, bx, by, os_, or_,
):
    chan = lax.axis_index("chan")
    s = lax.axis_index("slab")
    z = chan // NXC
    x = chan % NXC
    sib = 1 - s

    def at(zz, xx):
        return lax.rem(zz + 2 * NZC, NZC) * NXC + lax.rem(xx + 2 * NXC, NXC)

    barrier = pltpu.get_barrier_semaphore()
    peers = [(at(z, x), sib)]
    for k in range(1, NXC):
        peers += [(at(z, x + k), s), (at(z, x + k), sib)]
    for k in range(1, NZC):
        peers.append((at(z + k, x), s))
    for c, d in peers:
        pl.semaphore_signal(
            barrier, inc=1, device_id={"chan": c, "slab": d}, device_id_type=MESH
        )

    n = iota((1, 512), 1)
    quarter, yy, zz = n // 128, (n % 128) // 16, n % 16
    main_src = yy * 64 + quarter * 16 + zz
    halo_src = yy * 64 + (quarter * 16 + jnp.where(zz < 8, -1, 16) + 64) % 64
    m = iota((512, 512), 0)
    perm[:, 0:512] = (m == main_src).astype(F32).astype(BF)
    perm[:, 512:1024] = (m == halo_src).astype(F32).astype(BF)

    lane = iota((16, 128), 1)
    halo = [jnp.zeros((16, 128), F32) for _ in range(NXC)]
    for t, ref in ((0, g_ref), (1, x_ref)):
        moved = jnp.dot(ref[...], perm[...], preferred_element_type=F32)
        for p in range(4):
            keep = lane % 8 == (s + t) % 2 * 4 + p
            for q in range(NXC):
                rows = moved[16 * p : 16 * p + 16]
                part[q, 5 * t + p] = rows[:, 128 * q : 128 * q + 128].astype(BF)
                halo[q] = halo[q] + jnp.where(
                    keep, rows[:, 512 + 128 * q : 640 + 128 * q], 0.0
                )
    for q in range(NXC):
        part[q, 4] = halo[q].astype(BF)

    pl.semaphore_wait(barrier, len(peers))

    my_rows = pl.ds(pl.multiple_of(chan * 16, 16), 16)
    span = (pl.ds(0, 5), pl.ds(5, 4))
    waits = []
    own = pltpu.make_async_copy(part.at[x], acts.at[s, :, my_rows], loc_sem.at[0])
    own.start()
    for i in range(2):
        for k in (1, 3, 2):
            dest = lax.rem(x + k, NXC)
            copy = remote(
                part.at[dest, span[i]], acts.at[s, span[i], my_rows],
                xs.at[k - 1, i], xr.at[k - 1, i], at(z, dest), s,
            )
            copy.start()
            waits.append(copy)

    half = pl.ds(pl.multiple_of(s * 256, 128), 256)
    low = pl.ds(pl.multiple_of(s * 256, 128), 128)
    high = pl.ds(pl.multiple_of(s * 256 + 128, 128), 128)

    def wrow(k):
        return pl.ds(pl.multiple_of(lax.rem(x + k + NXC, NXC) * 16, 16), 16)

    own_w = pltpu.make_async_copy(
        w_ref.at[:, :, half], wbwd.at[:, wrow(0), half], loc_sem.at[1]
    )
    own_w.start()
    for i, k in enumerate((1, -1)):
        copy = remote(
            w_ref.at[:, :, half], wbwd.at[:, wrow(0), half],
            bs.at[i], br.at[i], at(z, x + k), s,
        )
        copy.start()
        waits.append(copy)

    n = iota((1, 256), 1)
    v, j, c = n // 128, (n % 128) // 32, n % 32
    permw[...] = (iota((512, 256), 0) == j * 128 + (2 * v + s) * 32 + c).astype(F32).astype(BF)
    for o in range(28):
        for t in range(4):
            at_rows, at_lanes = pl.ds(o // 4 * 16, 16), pl.ds(o % 4 * 128, 128)
            if o < 27:
                wl[t, at_rows, at_lanes] = w_ref[o, :, 128 * t : 128 * t + 128]
            else:
                wl[t, at_rows, at_lanes] = jnp.zeros((16, 128), BF)
    for t in range(4):
        packed = jnp.dot(wl[t], permw[...], preferred_element_type=F32).astype(BF)
        for v in range(2):
            for g in range(7):
                wpack[2 * t + v, g] = packed[16 * g : 16 * g + 16, 128 * v : 128 * v + 128]
    own_f = pltpu.make_async_copy(wpack.at[z], wrecv.at[:, z, x], loc_sem.at[2])
    own_f.start()
    for k in (4, 3, 5, 2, 6, 1, 7):
        dest = lax.rem(z + k, NZC)
        copy = remote(
            wpack.at[dest], wrecv.at[:, z, x], ws.at[k - 1], wr.at[k - 1], at(dest, x), s
        )
        copy.start()
        waits.append(copy)

    def block(k):
        return pl.ds(pl.multiple_of(lax.rem(z + k + NZC, NZC) * 64, 64), 64)

    def pass_on(k, i, direction, hop):
        ref = acts.at[s, span[i], block(k)]
        if direction is not None:
            step = 1 if direction == 0 else -1
            copy = remote(
                ref, ref, zs.at[direction, hop, i], zr.at[direction, hop, i],
                at(z + step, x), s,
            )
            copy.start()
            waits.append(copy)
        return ref

    def to_sibling(k, i):
        ref = acts.at[s, span[i], block(k)]
        copy = remote(
            ref, ref, ss.at[(k + NZC) % NZC, i], sr.at[(k + NZC) % NZC, i], at(z, x), sib
        )
        copy.start()
        waits.append(copy)

    own.wait()
    for i in range(2):
        for k in (1, 3, 2):
            source = lax.rem(x - k + NXC, NXC)
            rows = pl.ds(pl.multiple_of((z * NXC + source) * 16, 16), 16)
            arrived(acts.at[s, span[i], rows], xr.at[k - 1, i])
        pass_on(0, i, 0, 0)
        pass_on(0, i, 1, 0)
        to_sibling(0, i)

    def hop(h):
        for i in range(2):
            for direction in range(2):
                if h == 4 and i != direction:
                    continue
                k = -h if direction == 0 else h
                ref = acts.at[s, span[i], block(k)]
                arrived(ref, zr.at[direction, h - 1, i])
                if h < 3 or (h == 3 and i == direction):
                    pass_on(k, i, direction, h)
                to_sibling(k, i)

    hop(1)

    own_w.wait()
    for i, (k, to, lanes) in enumerate(((-1, 1, low), (1, -1, high))):
        arrived(wbwd.at[:, wrow(k), half], br.at[i])
        copy = remote(
            wbwd.at[:, wrow(k), lanes], wbwd.at[:, wrow(k), lanes],
            bs.at[2 + i], br.at[2 + i], at(z, x + to), s,
        )
        copy.start()
        waits.append(copy)

    own_f.wait()
    for k in range(1, NZC):
        source = lax.rem(z - k + NZC, NZC)
        arrived(wrecv.at[:, source, x], wr.at[k - 1])
    for i, k in enumerate((1, -1)):
        ref = wrecv.at[:, :, x]
        copy = remote(ref, ref, fs.at[i], fr.at[i], at(z, x + k), s)
        copy.start()
        waits.append(copy)

    hop(2)

    for i, (k, to) in enumerate(((-1, 1), (1, -1))):
        source = lax.rem(x + k + NXC, NXC)
        arrived(wrecv.at[:, :, source], fr.at[i])
        ref = wrecv.at[:, pl.ds(4 * i, 4), source]
        copy = remote(ref, ref, fs.at[2 + i], fr.at[2 + i], at(z, x + to), s)
        copy.start()
        waits.append(copy)
    for i, lanes in enumerate((low, high)):
        arrived(wbwd.at[:, wrow(2), lanes], br.at[2 + i])
    theirs = pl.ds(pl.multiple_of(sib * 32, 32), 32)
    mine = pl.ds(pl.multiple_of(s * 32, 32), 32)
    swap = remote(
        wbwd.at[:, theirs, half], wbwd.at[:, theirs, half], bx.at[0], by.at[0], at(z, x), sib
    )
    swap.start()
    waits.append(swap)

    hop(3)
    hop(4)

    other = pl.ds(pl.multiple_of(sib * 256, 128), 256)
    arrived(wbwd.at[:, mine, other], by.at[0])
    for i in range(2):
        for k in range(NZC):
            arrived(acts.at[sib, span[i], block(k)], sr.at[k, i])

    lane_z = iota((32, 128), 1) % 16
    lane_k = iota((512, 128), 1) % 8

    def conv(weights_of, t):
        sign = 1 if t == 0 else -1
        first, second = (0, 1) if t == 0 else (1, 0)
        edge = jnp.where(lane_k < 4, acts[first, 4], acts[second, 4])
        for ai in range(3):
            hprod[ai] = jnp.dot(weights_of(ai), edge, preferred_element_type=F32)

        def over_y(read, ci):
            total = read(3 + ci)
            for bi in (0, 2):
                shift = (16 * (bi - 1) * sign) % 128
                total = total + pltpu.roll(read(3 * bi + ci), shift, 1)
            return total

        edges = {}
        for ai in range(3):
            for ci in (0, 2):
                edges[ai, ci] = over_y(lambda r: hprod[ai, 32 * r : 32 * r + 32], ci)
        for pair in range(4):
            total = None
            for ai in range(3):
                planes = [(2 * pair + i - sign * (ai - 1)) % 8 for i in range(2)]
                both = jnp.concatenate(
                    [acts[p // 4, 5 * t + p % 4] for p in planes], axis=1
                )
                term = jnp.dot(weights_of(ai), both, preferred_element_type=F32)
                total = term if total is None else total + term
            for i in range(2):
                plane = 2 * pair + i
                cells = total[:, 128 * i : 128 * i + 128]

                def read(r):
                    return cells[32 * r : 32 * r + 32]

                result = over_y(read, 1)
                for ci in (0, 2):
                    e = sign * (ci - 1)
                    moved = pltpu.roll(over_y(read, ci), e % 128, 1)
                    outside = None
                    for ai in range(3):
                        source = (plane - sign * (ai - 1) + 4 * t) % 8
                        shift = (-source if e == 1 else 7 - source) % 128
                        term = edges[ai, ci]
                        if shift:
                            term = pltpu.roll(term, shift, 1)
                        outside = term if outside is None else outside + term
                    border = lane_z == (0 if e == 1 else 15)
                    result = result + jnp.where(border, outside, moved)
                result = result.astype(BF)
                for j in range(2):
                    outs[t, j, plane] = result[16 * j : 16 * j + 16]

        for j in range(2):
            for to in range(2):
                owner = 2 * s + j
                src = outs.at[t, j, pl.ds(4 * to, 4)]
                dst = outr.at[t, x]
                itself = jnp.logical_and(owner == x, s == to)

                @pl.when(itself)
                def _():
                    pltpu.make_async_copy(src, dst, or_.at[t, x]).start()

                @pl.when(jnp.logical_not(itself))
                def _():
                    remote(
                        src, dst, os_.at[t, j, to], or_.at[t, x], at(z, owner), to
                    ).start()

    def bwd_rows(ai):
        return wbwd[9 * ai : 9 * ai + 9, mine, :].reshape(288, 512)

    conv(bwd_rows, 0)

    for i in range(2):
        source = lax.rem(x + 2, NXC)
        arrived(wrecv.at[:, pl.ds(4 * i, 4), source], fr.at[2 + i])
    for g in range(7):
        wfwd[128 * g : 128 * g + 128, :] = wrecv[g].reshape(512, 128).T

    conv(lambda ai: wfwd[288 * ai : 288 * ai + 288, :], 1)

    for t, ref in ((0, go_ref), (1, co_ref)):
        for q in range(NXC):
            arrived(outr.at[t, q], or_.at[t, q])
        joined = jnp.concatenate(
            [outr[t, q].reshape(64, 128) for q in range(NXC)], axis=1
        )
        ref[...] = lax.dot_general(
            joined, perm[:, 0:512], (((1,), (1,)), ((), ())), preferred_element_type=F32
        ).astype(BF)

    for copy in waits:
        copy.wait_send()
    for t in range(2):
        for j in range(2):
            for to in range(2):
                owner = 2 * s + j

                @pl.when(jnp.logical_not(jnp.logical_and(owner == x, s == to)))
                def _():
                    remote(
                        outs.at[t, j, pl.ds(4 * to, 4)], outr.at[t, x],
                        os_.at[t, j, to], or_.at[t, x], at(z, owner), to,
                    ).wait_send()


def per_device(inputs, weights, out_grad):
    chans, slab_len, plane_size = inputs.shape

    def rows(block):
        return block.transpose(1, 0, 2).reshape(slab_len * chans, plane_size)

    vmem = pl.BlockSpec(memory_space=pltpu.VMEM)
    shape = jax.ShapeDtypeStruct((slab_len * chans, plane_size), BF)
    dma = pltpu.SemaphoreType.DMA
    grad, conv = pl.pallas_call(
        kernel,
        out_shape=(shape, shape),
        in_specs=[vmem] * 3,
        out_specs=(vmem, vmem),
        scratch_shapes=[
            pltpu.VMEM((512, 1024), BF),
            pltpu.VMEM((512, 256), BF),
            pltpu.VMEM((4, 9, 16, 128), BF),
            pltpu.VMEM((2, 9, 512, 128), BF),
            pltpu.VMEM((4, 112, 512), BF),
            pltpu.VMEM((8, 7, 16, 128), BF),
            pltpu.VMEM((7, 8, 4, 16, 128), BF),
            pltpu.VMEM((896, 512), BF),
            pltpu.VMEM((27, 64, 512), BF),
            pltpu.VMEM((2, 2, 8, 16, 128), BF),
            pltpu.VMEM((2, 4, 4, 16, 128), BF),
            pltpu.VMEM((3, 288, 128), F32),
            dma((3,)),
            dma((3, 2)), dma((3, 2)),
            dma((2, 4, 2)), dma((2, 4, 2)),
            dma((8, 2)), dma((8, 2)),
            dma((7,)), dma((7,)),
            dma((4,)), dma((4,)),
            dma((4,)), dma((4,)),
            dma((1,)), dma((1,)),
            dma((2, 2, 2)), dma((2, 4)),
        ],
        compiler_params=pltpu.CompilerParams(
            collective_id=0, has_side_effects=True, vmem_limit_bytes=48 * 1024 * 1024
        ),
    )(rows(out_grad), rows(inputs), weights)

    def back(block):
        return block.reshape(slab_len, chans, plane_size).transpose(1, 0, 2)

    return back(conv), back(grad)


def solution(mesh):
    act = P(("batch", "chan"), "slab", None)
    return jax.shard_map(
        per_device,
        mesh=mesh,
        in_specs=(act, P(None, "chan", None), act),
        out_specs=(act, act),
        check_vma=False,
    )
```

```python
import jax
import jax.numpy as jnp
from jax import lax
from jax.experimental import pallas as pl
from jax.experimental.pallas import tpu as pltpu
from jax.sharding import PartitionSpec as P

BF = jnp.bfloat16
F32 = jnp.float32
MESH = pl.DeviceIdType.MESH
NXC = 4
NYC = 4
NZC = 8


def remote(src, dst, send, recv, chan, slab, batch=None):
    where = {"chan": chan, "slab": slab}
    if batch is not None:
        where["batch"] = batch
    return pltpu.make_async_remote_copy(
        src_ref=src,
        dst_ref=dst,
        send_sem=send,
        recv_sem=recv,
        device_id=where,
        device_id_type=MESH,
    )


def arrived(ref, sem):
    pltpu.make_async_copy(ref, ref, sem).wait()


def iota(shape, dim):
    return lax.broadcasted_iota(jnp.int32, shape, dim)


def kernel(
    g_hbm, x_hbm, w_hbm, go_ref, co_ref,
    raw, tall, w_ref, in_sem,
    perm, permw, part, acts, wl, wpack, wrecv, wfwd, wbwd, outs, outr, hprod,
    loc_sem, xs, xr, zs, zr, ss, sr, ws, wr, fs, fr, fs2, fr2, yfs, yfr,
    bs, br, bs2, br2, ybs, ybr, bx, by, os_, or_,
):
    fetch = [
        pltpu.make_async_copy(src, dst, in_sem.at[i])
        for i, (src, dst) in enumerate(
            ((g_hbm, raw.at[0]), (x_hbm, raw.at[1]), (w_hbm, w_ref))
        )
    ]
    for copy in fetch:
        copy.start()
    chan = lax.axis_index("chan")
    s = lax.axis_index("slab")
    z = chan // NXC
    x = chan % NXC
    y = lax.axis_index("batch")
    sib = 1 - s
    par = lax.rem(y, 2)
    y_next = (lax.rem(y + 1, NYC), lax.rem(y + NYC - 1, NYC))

    def at(zz, xx):
        return lax.rem(zz + 2 * NZC, NZC) * NXC + lax.rem(xx + 2 * NXC, NXC)

    barrier = pltpu.get_barrier_semaphore()
    peers = [(at(z, x), sib)]
    for k in range(1, NXC):
        peers += [(at(z, x + k), s), (at(z, x + k), sib)]
    for k in range(1, NZC):
        peers.append((at(z + k, x), s))
    for c, d in peers:
        pl.semaphore_signal(
            barrier, inc=1, device_id={"chan": c, "slab": d}, device_id_type=MESH
        )
    for b in y_next:
        pl.semaphore_signal(
            barrier, inc=1, device_id={"chan": chan, "slab": s, "batch": b},
            device_id_type=MESH,
        )

    n = iota((1, 512), 1)
    quarter, yy, zz = n // 128, (n % 128) // 16, n % 16
    main_src = yy * 64 + quarter * 16 + zz
    halo_src = yy * 64 + (quarter * 16 + jnp.where(zz < 8, -1, 16) + 64) % 64
    m = iota((512, 512), 0)
    perm[:, 0:512] = (m == main_src).astype(F32).astype(BF)
    perm[:, 512:1024] = (m == halo_src).astype(F32).astype(BF)

    lane = iota((16, 128), 1)
    halo = [jnp.zeros((16, 128), F32) for _ in range(NXC)]
    for t in range(2):
        fetch[t].wait()
        for i in range(16):
            for v in range(4):
                tall[4 * t + v, 4 * i : 4 * i + 4] = raw[
                    t, i, :, 128 * v : 128 * v + 128
                ].astype(F32)
        planes = [
            jnp.concatenate(
                [tall[4 * t + v, pl.ds(p, 16, stride=4)] for v in range(4)], axis=1
            )
            for p in range(4)
        ]
        moved = jnp.dot(
            jnp.concatenate(planes, axis=0).astype(BF), perm[...], preferred_element_type=F32
        )
        for p in range(4):
            keep = lane % 8 == (s + t) % 2 * 4 + p
            for q in range(NXC):
                rows = moved[16 * p : 16 * p + 16]
                part[q, 5 * t + p] = rows[:, 128 * q : 128 * q + 128].astype(BF)
                halo[q] = halo[q] + jnp.where(
                    keep, rows[:, 512 + 128 * q : 640 + 128 * q], 0.0
                )
    for q in range(NXC):
        part[q, 4] = halo[q].astype(BF)

    pl.semaphore_wait(barrier, len(peers) + 2)

    my_rows = pl.ds(pl.multiple_of(chan * 16, 16), 16)
    span = (pl.ds(0, 5), pl.ds(5, 4))
    chunk = (pl.ds(0, 2), pl.ds(2, 3), pl.ds(5, 2), pl.ds(7, 2))
    waits = []
    own = pltpu.make_async_copy(part.at[x], acts.at[s, :, my_rows], loc_sem.at[0])
    own.start()
    for i in range(2):
        for k in (1, 3, 2):
            dest = lax.rem(x + k, NXC)
            copy = remote(
                part.at[dest, span[i]], acts.at[s, span[i], my_rows],
                xs.at[k - 1, i], xr.at[k - 1, i], at(z, dest), s,
            )
            copy.start()
            waits.append(copy)

    half = pl.ds(pl.multiple_of(s * 256, 128), 256)
    here = pl.ds(pl.multiple_of(s * 256 + par * 128, 128), 128)
    there = pl.ds(pl.multiple_of(s * 256 + (1 - par) * 128, 128), 128)
    offsets = (pl.ds(0, 14), pl.ds(14, 13))

    def wrow(k):
        return pl.ds(pl.multiple_of(lax.rem(x + k + NXC, NXC) * 16, 16), 16)

    fetch[2].wait()
    own_w = pltpu.make_async_copy(
        w_ref.at[:, :, half], wbwd.at[:, wrow(0), half], loc_sem.at[1]
    )
    own_w.start()
    for h in range(2):
        for i, k in enumerate((1, -1)):
            copy = remote(
                w_ref.at[offsets[h], :, here], wbwd.at[offsets[h], wrow(0), here],
                bs.at[i, h], br.at[i, h], at(z, x + k), s,
            )
            copy.start()
            waits.append(copy)

    def w_along_y(j, k, h):
        ref = wbwd.at[offsets[h], wrow(k), here]
        copy = remote(ref, ref, ybs.at[j, h], ybr.at[j, h], chan, s, y_next[h])
        copy.start()
        waits.append(copy)

    n = iota((1, 256), 1)
    v, j, c = n // 128, (n % 128) // 32, n % 32
    permw[...] = (iota((512, 256), 0) == j * 128 + (2 * v + s) * 32 + c).astype(F32).astype(BF)
    for o in range(28):
        for t in range(4):
            at_rows, at_lanes = pl.ds(o // 4 * 16, 16), pl.ds(o % 4 * 128, 128)
            if o < 27:
                wl[t, at_rows, at_lanes] = w_ref[o, :, 128 * t : 128 * t + 128]
            else:
                wl[t, at_rows, at_lanes] = jnp.zeros((16, 128), BF)
    for t in range(4):
        packed = jnp.dot(wl[t], permw[...], preferred_element_type=F32).astype(BF)
        for v in range(2):
            for g in range(7):
                wpack[2 * t + v, g] = packed[16 * g : 16 * g + 16, 128 * v : 128 * v + 128]
    zmine = lax.rem(z, 2) == par

    def own_forward():
        return pltpu.make_async_copy(
            wpack.at[z], wrecv.at[:, z // 2, par, x], loc_sem.at[2]
        )

    def to_z(k):
        dest = lax.rem(z + k, NZC)
        return remote(
            wpack.at[dest], wrecv.at[:, z // 2, par, x], ws.at[k - 1], wr.at[k - 1],
            at(dest, x), s,
        )

    @pl.when(zmine)
    def _():
        own_forward().start()
        for k in (4, 3, 5, 2, 6, 1, 7):
            to_z(k).start()

    pairs = (pl.ds(0, 2), pl.ds(2, 2))

    def f_along_y(j, k, h):
        ref = wrecv.at[:, pairs[h], par, lax.rem(x + k + NXC, NXC)]
        copy = remote(ref, ref, yfs.at[j, h], yfr.at[j, h], chan, s, y_next[h])
        copy.start()
        waits.append(copy)

    def block(k):
        return pl.ds(pl.multiple_of(lax.rem(z + k + NZC, NZC) * 64, 64), 64)

    def pass_on(k, c, direction, hop):
        ref = acts.at[s, chunk[c], block(k)]
        copy = remote(
            ref, ref, zs.at[direction, hop, c], zr.at[direction, hop, c],
            at(z + (1 if direction == 0 else -1), x), s,
        )
        copy.start()
        waits.append(copy)

    def to_sibling(k, i):
        ref = acts.at[s, span[i], block(k)]
        copy = remote(
            ref, ref, ss.at[(k + NZC) % NZC, i], sr.at[(k + NZC) % NZC, i], at(z, x), sib
        )
        copy.start()
        waits.append(copy)

    own.wait()
    for i in range(2):
        for k in (1, 3, 2):
            source = lax.rem(x - k + NXC, NXC)
            rows = pl.ds(pl.multiple_of((z * NXC + source) * 16, 16), 16)
            arrived(acts.at[s, span[i], rows], xr.at[k - 1, i])
        for c in (2 * i, 2 * i + 1):
            pass_on(0, c, 0, 0)
            pass_on(0, c, 1, 0)
        to_sibling(0, i)

    def hop(h):
        for c in range(4):
            for direction in range(2):
                if h == 4 and c // 2 != direction:
                    continue
                k = -h if direction == 0 else h
                arrived(acts.at[s, chunk[c], block(k)], zr.at[direction, h - 1, c])
                if h < 3 or (h == 3 and c // 2 == direction):
                    pass_on(k, c, direction, h)
                if c % 2:
                    to_sibling(k, c // 2)

    own_w.wait()
    for h in range(2):
        for i, (k, to) in enumerate(((-1, 1), (1, -1))):
            ref = wbwd.at[offsets[h], wrow(k), here]
            arrived(ref, br.at[i, h])
            if i == h:
                copy = remote(ref, ref, bs2.at[i], br2.at[i], at(z, x + to), s)
                copy.start()
                waits.append(copy)
            w_along_y(i, k, h)

    @pl.when(zmine)
    def _():
        own_forward().wait()

    for k in range(1, NZC):
        source = lax.rem(z - k + NZC, NZC)

        @pl.when(lax.rem(source, 2) == par)
        def _():
            arrived(wrecv.at[:, source // 2, par, x], wr.at[k - 1])

    for h in range(2):
        for i, k in enumerate((1, -1)):
            ref = wrecv.at[:, pairs[h], par, x]
            copy = remote(ref, ref, fs.at[i, h], fr.at[i, h], at(z, x + k), s)
            copy.start()
            waits.append(copy)
        f_along_y(2, 0, h)

    hop(1)

    for h in range(2):
        arrived(wbwd.at[offsets[h], wrow(2), here], br2.at[h])
        w_along_y(2, 2, h)
    for h in range(2):
        for i, (k, to) in enumerate(((-1, 1), (1, -1))):
            ref = wrecv.at[:, pairs[h], par, lax.rem(x + k + NXC, NXC)]
            arrived(ref, fr.at[i, h])
            if i == h:
                copy = remote(ref, ref, fs2.at[i], fr2.at[i], at(z, x + to), s)
                copy.start()
                waits.append(copy)
            f_along_y(i, k, h)

    hop(2)

    for h in range(2):
        arrived(wrecv.at[:, pairs[h], par, lax.rem(x + 2, NXC)], fr2.at[h])
        f_along_y(3, 2, h)
    for h in range(2):
        for j, k in enumerate((-1, 1, 2)):
            arrived(wbwd.at[offsets[h], wrow(k), there], ybr.at[j, h])
    theirs = pl.ds(pl.multiple_of(sib * 32, 32), 32)
    mine = pl.ds(pl.multiple_of(s * 32, 32), 32)
    swap = remote(
        wbwd.at[:, theirs, half], wbwd.at[:, theirs, half], bx.at[0], by.at[0], at(z, x), sib
    )
    swap.start()
    waits.append(swap)

    hop(3)
    hop(4)

    other = pl.ds(pl.multiple_of(sib * 256, 128), 256)
    arrived(wbwd.at[:, mine, other], by.at[0])
    for i in range(2):
        for k in range(NZC):
            arrived(acts.at[sib, span[i], block(k)], sr.at[k, i])

    lane_z = iota((32, 128), 1) % 16
    lane_k = iota((512, 128), 1) % 8

    def send_out(t, to):
        for j in range(2):
            owner = 2 * s + j
            src = outs.at[t, j, pl.ds(4 * to, 4)]
            dst = outr.at[t, x]
            itself = jnp.logical_and(owner == x, s == to)

            @pl.when(itself)
            def _():
                pltpu.make_async_copy(src, dst, or_.at[t, x]).start()

            @pl.when(jnp.logical_not(itself))
            def _():
                remote(
                    src, dst, os_.at[t, j, to], or_.at[t, x], at(z, owner), to
                ).start()

    def conv(weights_of, t):
        sign = 1 if t == 0 else -1
        first, second = (0, 1) if t == 0 else (1, 0)
        edge = jnp.where(lane_k < 4, acts[first, 4], acts[second, 4])
        for ai in range(3):
            hprod[ai] = jnp.dot(weights_of(ai), edge, preferred_element_type=F32)

        def over_y(read, ci):
            total = read(3 + ci)
            for bi in (0, 2):
                shift = (16 * (bi - 1) * sign) % 128
                total = total + pltpu.roll(read(3 * bi + ci), shift, 1)
            return total

        edges = {}
        for ai in range(3):
            for ci in (0, 2):
                edges[ai, ci] = over_y(lambda r: hprod[ai, 32 * r : 32 * r + 32], ci)
        for pair in range(4):
            total = None
            for ai in range(3):
                planes = [(2 * pair + i - sign * (ai - 1)) % 8 for i in range(2)]
                both = jnp.concatenate(
                    [acts[p // 4, 5 * t + p % 4] for p in planes], axis=1
                )
                term = jnp.dot(weights_of(ai), both, preferred_element_type=F32)
                total = term if total is None else total + term
            for i in range(2):
                plane = 2 * pair + i
                cells = total[:, 128 * i : 128 * i + 128]

                def read(r):
                    return cells[32 * r : 32 * r + 32]

                result = over_y(read, 1)
                for ci in (0, 2):
                    e = sign * (ci - 1)
                    moved = pltpu.roll(over_y(read, ci), e % 128, 1)
                    outside = None
                    for ai in range(3):
                        source = (plane - sign * (ai - 1) + 4 * t) % 8
                        shift = (-source if e == 1 else 7 - source) % 128
                        term = edges[ai, ci]
                        if shift:
                            term = pltpu.roll(term, shift, 1)
                        outside = term if outside is None else outside + term
                    border = lane_z == (0 if e == 1 else 15)
                    result = result + jnp.where(border, outside, moved)
                result = result.astype(BF)
                for j in range(2):
                    outs[t, j, plane] = result[16 * j : 16 * j + 16]
            if pair % 2:
                send_out(t, pair // 2)

    def bwd_rows(ai):
        return wbwd[9 * ai : 9 * ai + 9, mine, :].reshape(288, 512)

    conv(bwd_rows, 0)

    for h in range(2):
        for j, k in enumerate((-1, 1, 0, 2)):
            column = lax.rem(x + k + NXC, NXC)
            arrived(wrecv.at[:, pairs[h], 1 - par, column], yfr.at[j, h])
    for g in range(7):
        wfwd[128 * g : 128 * g + 128, :] = wrecv[g].reshape(512, 128).T

    conv(lambda ai: wfwd[288 * ai : 288 * ai + 288, :], 1)

    for t, ref in ((0, go_ref), (1, co_ref)):
        for q in range(NXC):
            arrived(outr.at[t, q], or_.at[t, q])
        joined = jnp.concatenate(
            [outr[t, q].reshape(64, 128) for q in range(NXC)], axis=1
        )
        ref[...] = lax.dot_general(
            joined, perm[:, 0:512], (((1,), (1,)), ((), ())), preferred_element_type=F32
        ).astype(BF)

    for copy in waits:
        copy.wait_send()

    @pl.when(zmine)
    def _():
        for k in range(1, NZC):
            to_z(k).wait_send()

    for t in range(2):
        for j in range(2):
            for to in range(2):
                owner = 2 * s + j

                @pl.when(jnp.logical_not(jnp.logical_and(owner == x, s == to)))
                def _():
                    remote(
                        outs.at[t, j, pl.ds(4 * to, 4)], outr.at[t, x],
                        os_.at[t, j, to], or_.at[t, x], at(z, owner), to,
                    ).wait_send()


def per_device(inputs, weights, out_grad):
    chans, slab_len, plane_size = inputs.shape

    vmem = pl.BlockSpec(memory_space=pltpu.VMEM)
    shape = jax.ShapeDtypeStruct((slab_len * chans, plane_size), BF)
    dma = pltpu.SemaphoreType.DMA
    grad, conv = pl.pallas_call(
        kernel,
        out_shape=(shape, shape),
        in_specs=[pl.BlockSpec(memory_space=pl.ANY)] * 3,
        out_specs=(vmem, vmem),
        scratch_shapes=[
            pltpu.VMEM((2, 16, 4, 512), BF),
            pltpu.VMEM((8, 64, 128), F32),
            pltpu.VMEM((27, 16, 512), BF),
            dma((3,)),
            pltpu.VMEM((512, 1024), BF),
            pltpu.VMEM((512, 256), BF),
            pltpu.VMEM((4, 9, 16, 128), BF),
            pltpu.VMEM((2, 9, 512, 128), BF),
            pltpu.VMEM((4, 112, 512), BF),
            pltpu.VMEM((8, 7, 16, 128), BF),
            pltpu.VMEM((7, 4, 2, 4, 16, 128), BF),
            pltpu.VMEM((896, 512), BF),
            pltpu.VMEM((27, 64, 512), BF),
            pltpu.VMEM((2, 2, 8, 16, 128), BF),
            pltpu.VMEM((2, 4, 4, 16, 128), BF),
            pltpu.VMEM((3, 288, 128), F32),
            dma((3,)),
            dma((3, 2)), dma((3, 2)),
            dma((2, 4, 4)), dma((2, 4, 4)),
            dma((8, 2)), dma((8, 2)),
            dma((7,)), dma((7,)),
            dma((2, 2)), dma((2, 2)), dma((2,)), dma((2,)), dma((4, 2)), dma((4, 2)),
            dma((2, 2)), dma((2, 2)), dma((2,)), dma((2,)), dma((3, 2)), dma((3, 2)),
            dma((1,)), dma((1,)),
            dma((2, 2, 2)), dma((2, 4)),
        ],
        compiler_params=pltpu.CompilerParams(
            collective_id=0, has_side_effects=True, vmem_limit_bytes=60 * 1024 * 1024
        ),
    )(out_grad, inputs, weights)

    def back(block):
        return block.reshape(slab_len, chans, plane_size).transpose(1, 0, 2)

    return back(conv), back(grad)


def solution(mesh):
    act = P(("batch", "chan"), "slab", None)
    return jax.shard_map(
        per_device,
        mesh=mesh,
        in_specs=(act, P(None, "chan", None), act),
        out_specs=(act, act),
        check_vma=False,
    )
```

```python
import jax
import jax.numpy as jnp
from jax import lax
from jax.experimental import pallas as pl
from jax.experimental.pallas import tpu as pltpu
from jax.sharding import PartitionSpec as P

BF = jnp.bfloat16
F32 = jnp.float32
MESH = pl.DeviceIdType.MESH
NXC = 4
NYC = 4
NZC = 8


def remote(src, dst, send, recv, chan, slab, batch=None):
    where = {"chan": chan, "slab": slab}
    if batch is not None:
        where["batch"] = batch
    return pltpu.make_async_remote_copy(
        src_ref=src,
        dst_ref=dst,
        send_sem=send,
        recv_sem=recv,
        device_id=where,
        device_id_type=MESH,
    )


def arrived(ref, sem):
    pltpu.make_async_copy(ref, ref, sem).wait()


def iota(shape, dim):
    return lax.broadcasted_iota(jnp.int32, shape, dim)


def kernel(
    g_hbm, x_hbm, w_hbm, go_ref, co_ref,
    raw, tall, w_ref, in_sem,
    perm, permw, part, acts, wl, wpack, wrecv, wfwd, wbwd, outs, outr, hprod,
    loc_sem, xs, xr, zs, zr, ss, sr, ws, wr, fs, fr, yfs, yfr,
    bs, br, ybs, ybr, bx, by, os_, or_,
):
    fetch = [
        pltpu.make_async_copy(src, dst, in_sem.at[i])
        for i, (src, dst) in enumerate(
            ((g_hbm, raw.at[0]), (x_hbm, raw.at[1]), (w_hbm, w_ref))
        )
    ]
    for copy in fetch:
        copy.start()
    chan = lax.axis_index("chan")
    s = lax.axis_index("slab")
    z = chan // NXC
    x = chan % NXC
    y = lax.axis_index("batch")
    sib = 1 - s
    par = lax.rem(y, 2)
    y_next = (lax.rem(y + 1, NYC), lax.rem(y + NYC - 1, NYC))

    def at(zz, xx):
        return lax.rem(zz + 2 * NZC, NZC) * NXC + lax.rem(xx + 2 * NXC, NXC)

    barrier = pltpu.get_barrier_semaphore()
    peers = [(at(z, x), sib)]
    for k in range(1, NXC):
        peers += [(at(z, x + k), s), (at(z, x + k), sib)]
    for k in range(1, NZC):
        peers.append((at(z + k, x), s))
    for c, d in peers:
        pl.semaphore_signal(
            barrier, inc=1, device_id={"chan": c, "slab": d}, device_id_type=MESH
        )
    for b in y_next:
        pl.semaphore_signal(
            barrier, inc=1, device_id={"chan": chan, "slab": s, "batch": b},
            device_id_type=MESH,
        )

    n = iota((1, 512), 1)
    quarter, yy, zz = n // 128, (n % 128) // 16, n % 16
    main_src = yy * 64 + quarter * 16 + zz
    halo_src = yy * 64 + (quarter * 16 + jnp.where(zz < 8, -1, 16) + 64) % 64
    m = iota((512, 512), 0)
    perm[:, 0:512] = (m == main_src).astype(F32).astype(BF)
    perm[:, 512:1024] = (m == halo_src).astype(F32).astype(BF)

    lane = iota((16, 128), 1)
    halo = [jnp.zeros((16, 128), F32) for _ in range(NXC)]
    for t in range(2):
        fetch[t].wait()
        for i in range(16):
            for v in range(4):
                tall[4 * t + v, 4 * i : 4 * i + 4] = raw[
                    t, i, :, 128 * v : 128 * v + 128
                ].astype(F32)
        planes = [
            jnp.concatenate(
                [tall[4 * t + v, pl.ds(p, 16, stride=4)] for v in range(4)], axis=1
            )
            for p in range(4)
        ]
        moved = jnp.dot(
            jnp.concatenate(planes, axis=0).astype(BF), perm[...], preferred_element_type=F32
        )
        for p in range(4):
            keep = lane % 8 == (s + t) % 2 * 4 + p
            for q in range(NXC):
                rows = moved[16 * p : 16 * p + 16]
                part[q, 5 * t + p] = rows[:, 128 * q : 128 * q + 128].astype(BF)
                halo[q] = halo[q] + jnp.where(
                    keep, rows[:, 512 + 128 * q : 640 + 128 * q], 0.0
                )
    for q in range(NXC):
        part[q, 4] = halo[q].astype(BF)

    pl.semaphore_wait(barrier, len(peers) + 2)

    my_rows = pl.ds(pl.multiple_of(chan * 16, 16), 16)
    span = (pl.ds(0, 5), pl.ds(5, 4))
    chunk = (pl.ds(0, 2), pl.ds(2, 3), pl.ds(5, 2), pl.ds(7, 2))
    waits = []
    own = pltpu.make_async_copy(part.at[x], acts.at[s, :, my_rows], loc_sem.at[0])
    own.start()
    for i in range(2):
        for k in (1, 3, 2):
            dest = lax.rem(x + k, NXC)
            copy = remote(
                part.at[dest, span[i]], acts.at[s, span[i], my_rows],
                xs.at[k - 1, i], xr.at[k - 1, i], at(z, dest), s,
            )
            copy.start()
            waits.append(copy)

    half = pl.ds(pl.multiple_of(s * 256, 128), 256)
    here = pl.ds(pl.multiple_of(s * 256 + par * 128, 128), 128)
    there = pl.ds(pl.multiple_of(s * 256 + (1 - par) * 128, 128), 128)
    offsets = (pl.ds(0, 14), pl.ds(14, 13))

    def wrow(k):
        return pl.ds(pl.multiple_of(lax.rem(x + k + NXC, NXC) * 16, 16), 16)

    fetch[2].wait()
    own_w = pltpu.make_async_copy(
        w_ref.at[:, :, half], wbwd.at[:, wrow(0), half], loc_sem.at[1]
    )
    own_w.start()
    for k in (1, 3, 2):
        copy = remote(
            w_ref.at[:, :, here], wbwd.at[:, wrow(0), here],
            bs.at[k - 1], br.at[k - 1], at(z, x + k), s,
        )
        copy.start()
        waits.append(copy)

    def w_along_y(k, h):
        ref = wbwd.at[offsets[h], wrow(-k), here]
        copy = remote(ref, ref, ybs.at[k - 1, h], ybr.at[k - 1, h], chan, s, y_next[h])
        copy.start()
        waits.append(copy)

    n = iota((1, 256), 1)
    v, j, c = n // 128, (n % 128) // 32, n % 32
    permw[...] = (iota((512, 256), 0) == j * 128 + (2 * v + s) * 32 + c).astype(F32).astype(BF)
    for o in range(28):
        for t in range(4):
            at_rows, at_lanes = pl.ds(o // 4 * 16, 16), pl.ds(o % 4 * 128, 128)
            if o < 27:
                wl[t, at_rows, at_lanes] = w_ref[o, :, 128 * t : 128 * t + 128]
            else:
                wl[t, at_rows, at_lanes] = jnp.zeros((16, 128), BF)
    for t in range(4):
        packed = jnp.dot(wl[t], permw[...], preferred_element_type=F32).astype(BF)
        for v in range(2):
            for g in range(7):
                wpack[2 * t + v, g] = packed[16 * g : 16 * g + 16, 128 * v : 128 * v + 128]
    zmine = lax.rem(z, 2) == par

    def own_forward():
        return pltpu.make_async_copy(
            wpack.at[z], wrecv.at[:, z // 2, par, x], loc_sem.at[2]
        )

    def to_z(k):
        dest = lax.rem(z + k, NZC)
        return remote(
            wpack.at[dest], wrecv.at[:, z // 2, par, x], ws.at[k - 1], wr.at[k - 1],
            at(dest, x), s,
        )

    @pl.when(zmine)
    def _():
        own_forward().start()
        for k in (4, 3, 5, 2, 6, 1, 7):
            to_z(k).start()

    pairs = (pl.ds(0, 2), pl.ds(2, 2))

    def f_along_y(k, h):
        ref = wrecv.at[:, pairs[h], par, lax.rem(x - k + NXC, NXC)]
        copy = remote(ref, ref, yfs.at[k, h], yfr.at[k, h], chan, s, y_next[h])
        copy.start()
        waits.append(copy)

    def block(k):
        return pl.ds(pl.multiple_of(lax.rem(z + k + NZC, NZC) * 64, 64), 64)

    def pass_on(k, c, direction, hop):
        ref = acts.at[s, chunk[c], block(k)]
        copy = remote(
            ref, ref, zs.at[direction, hop, c], zr.at[direction, hop, c],
            at(z + (1 if direction == 0 else -1), x), s,
        )
        copy.start()
        waits.append(copy)

    def to_sibling(k, i):
        ref = acts.at[s, span[i], block(k)]
        copy = remote(
            ref, ref, ss.at[(k + NZC) % NZC, i], sr.at[(k + NZC) % NZC, i], at(z, x), sib
        )
        copy.start()
        waits.append(copy)

    own.wait()
    for i in range(2):
        for k in (1, 3, 2):
            source = lax.rem(x - k + NXC, NXC)
            rows = pl.ds(pl.multiple_of((z * NXC + source) * 16, 16), 16)
            arrived(acts.at[s, span[i], rows], xr.at[k - 1, i])
        for c in (2 * i, 2 * i + 1):
            pass_on(0, c, 0, 0)
            pass_on(0, c, 1, 0)
        to_sibling(0, i)

    def hop(h):
        for c in range(4):
            for direction in range(2):
                if h == 4 and c % 2 != direction:
                    continue
                k = -h if direction == 0 else h
                arrived(acts.at[s, chunk[c], block(k)], zr.at[direction, h - 1, c])
                if h < 3 or (h == 3 and c % 2 == direction):
                    pass_on(k, c, direction, h)
                if c % 2:
                    to_sibling(4 if h == 4 else k, c // 2)

    theirs = pl.ds(pl.multiple_of(sib * 32, 32), 32)
    mine = pl.ds(pl.multiple_of(s * 32, 32), 32)

    def back_x():
        own_w.wait()
        for k in (1, 3, 2):
            arrived(wbwd.at[:, wrow(-k), here], br.at[k - 1])
            for h in range(2):
                w_along_y(k, h)

    def forward_z():
        @pl.when(zmine)
        def _():
            own_forward().wait()

        for k in range(1, NZC):
            source = lax.rem(z - k + NZC, NZC)

            @pl.when(lax.rem(source, 2) == par)
            def _():
                arrived(wrecv.at[:, source // 2, par, x], wr.at[k - 1])

        for k in (1, 3, 2):
            ref = wrecv.at[:, :, par, x]
            copy = remote(ref, ref, fs.at[k - 1], fr.at[k - 1], at(z, x + k), s)
            copy.start()
            waits.append(copy)
        for h in range(2):
            f_along_y(0, h)

    def forward_x():
        for k in (1, 3, 2):
            arrived(wrecv.at[:, :, par, lax.rem(x - k + NXC, NXC)], fr.at[k - 1])
            for h in range(2):
                f_along_y(k, h)

    def back_y():
        for h in range(2):
            for k in (1, 3, 2):
                arrived(wbwd.at[offsets[h], wrow(-k), there], ybr.at[k - 1, h])
        swap = remote(
            wbwd.at[:, theirs, half], wbwd.at[:, theirs, half], bx.at[0], by.at[0], at(z, x), sib
        )
        swap.start()
        waits.append(swap)

    back_x()
    hop(1)
    forward_z()
    hop(2)
    forward_x()
    hop(3)
    back_y()
    hop(4)

    other = pl.ds(pl.multiple_of(sib * 256, 128), 256)
    arrived(wbwd.at[:, mine, other], by.at[0])

    def from_sibling(i):
        for k in range(NZC):
            arrived(acts.at[sib, span[i], block(k)], sr.at[k, i])

    from_sibling(0)

    lane_z = iota((32, 128), 1) % 16
    lane_k = iota((512, 128), 1) % 8

    def send_out(t, to):
        for j in range(2):
            owner = 2 * s + j
            src = outs.at[t, j, pl.ds(4 * to, 4)]
            dst = outr.at[t, x]
            itself = jnp.logical_and(owner == x, s == to)

            @pl.when(itself)
            def _():
                pltpu.make_async_copy(src, dst, or_.at[t, x]).start()

            @pl.when(jnp.logical_not(itself))
            def _():
                remote(
                    src, dst, os_.at[t, j, to], or_.at[t, x], at(z, owner), to
                ).start()

    def conv_of(weights_of, t):
        sign = 1 if t == 0 else -1
        first, second = (0, 1) if t == 0 else (1, 0)
        edge = jnp.where(lane_k < 4, acts[first, 4], acts[second, 4])
        for ai in range(3):
            hprod[3 * t + ai] = jnp.dot(weights_of(ai), edge, preferred_element_type=F32)

        def over_y(read, ci):
            total = read(3 + ci)
            for bi in (0, 2):
                shift = (16 * (bi - 1) * sign) % 128
                total = total + pltpu.roll(read(3 * bi + ci), shift, 1)
            return total

        edges = {}
        for ai in range(3):
            for ci in (0, 2):
                edges[ai, ci] = over_y(lambda r: hprod[3 * t + ai, 32 * r : 32 * r + 32], ci)
        def planes_of(to):
            for pair in (2 * to, 2 * to + 1):
                total = None
                for ai in range(3):
                    planes = [(2 * pair + i - sign * (ai - 1)) % 8 for i in range(2)]
                    both = jnp.concatenate(
                        [acts[p // 4, 5 * t + p % 4] for p in planes], axis=1
                    )
                    term = jnp.dot(weights_of(ai), both, preferred_element_type=F32)
                    total = term if total is None else total + term
                for i in range(2):
                    plane = 2 * pair + i
                    cells = total[:, 128 * i : 128 * i + 128]

                    def read(r):
                        return cells[32 * r : 32 * r + 32]

                    result = over_y(read, 1)
                    for ci in (0, 2):
                        e = sign * (ci - 1)
                        moved = pltpu.roll(over_y(read, ci), e % 128, 1)
                        outside = None
                        for ai in range(3):
                            source = (plane - sign * (ai - 1) + 4 * t) % 8
                            shift = (-source if e == 1 else 7 - source) % 128
                            term = edges[ai, ci]
                            if shift:
                                term = pltpu.roll(term, shift, 1)
                            outside = term if outside is None else outside + term
                        border = lane_z == (0 if e == 1 else 15)
                        result = result + jnp.where(border, outside, moved)
                    result = result.astype(BF)
                    for j in range(2):
                        outs[t, j, plane] = result[16 * j : 16 * j + 16]
            send_out(t, to)

        return planes_of

    def bwd_rows(ai):
        return wbwd[9 * ai : 9 * ai + 9, mine, :].reshape(288, 512)

    back = conv_of(bwd_rows, 0)
    back(1)

    from_sibling(1)

    for h in range(2):
        for k in (0, 1, 3, 2):
            column = lax.rem(x - k + NXC, NXC)
            arrived(wrecv.at[:, pairs[h], 1 - par, column], yfr.at[k, h])
    for g in range(7):
        wfwd[128 * g : 128 * g + 128, :] = wrecv[g].reshape(512, 128).T

    forth = conv_of(lambda ai: wfwd[288 * ai : 288 * ai + 288, :], 1)
    forth(1)
    back(0)
    forth(0)

    for t, ref in ((0, go_ref), (1, co_ref)):
        for q in range(NXC):
            arrived(outr.at[t, q], or_.at[t, q])
        joined = jnp.concatenate(
            [outr[t, q].reshape(64, 128) for q in range(NXC)], axis=1
        )
        ref[...] = lax.dot_general(
            joined, perm[:, 0:512], (((1,), (1,)), ((), ())), preferred_element_type=F32
        ).astype(BF)

    for copy in waits:
        copy.wait_send()

    @pl.when(zmine)
    def _():
        for k in range(1, NZC):
            to_z(k).wait_send()

    for t in range(2):
        for j in range(2):
            for to in range(2):
                owner = 2 * s + j

                @pl.when(jnp.logical_not(jnp.logical_and(owner == x, s == to)))
                def _():
                    remote(
                        outs.at[t, j, pl.ds(4 * to, 4)], outr.at[t, x],
                        os_.at[t, j, to], or_.at[t, x], at(z, owner), to,
                    ).wait_send()


def per_device(inputs, weights, out_grad):
    chans, slab_len, plane_size = inputs.shape

    vmem = pl.BlockSpec(memory_space=pltpu.VMEM)
    shape = jax.ShapeDtypeStruct((slab_len * chans, plane_size), BF)
    dma = pltpu.SemaphoreType.DMA
    grad, conv = pl.pallas_call(
        kernel,
        out_shape=(shape, shape),
        in_specs=[pl.BlockSpec(memory_space=pl.ANY)] * 3,
        out_specs=(vmem, vmem),
        scratch_shapes=[
            pltpu.VMEM((2, 16, 4, 512), BF),
            pltpu.VMEM((8, 64, 128), F32),
            pltpu.VMEM((27, 16, 512), BF),
            dma((3,)),
            pltpu.VMEM((512, 1024), BF),
            pltpu.VMEM((512, 256), BF),
            pltpu.VMEM((4, 9, 16, 128), BF),
            pltpu.VMEM((2, 9, 512, 128), BF),
            pltpu.VMEM((4, 112, 512), BF),
            pltpu.VMEM((8, 7, 16, 128), BF),
            pltpu.VMEM((7, 4, 2, 4, 16, 128), BF),
            pltpu.VMEM((896, 512), BF),
            pltpu.VMEM((27, 64, 512), BF),
            pltpu.VMEM((2, 2, 8, 16, 128), BF),
            pltpu.VMEM((2, 4, 4, 16, 128), BF),
            pltpu.VMEM((6, 288, 128), F32),
            dma((3,)),
            dma((3, 2)), dma((3, 2)),
            dma((2, 4, 4)), dma((2, 4, 4)),
            dma((8, 2)), dma((8, 2)),
            dma((7,)), dma((7,)),
            dma((3,)), dma((3,)), dma((4, 2)), dma((4, 2)),
            dma((3,)), dma((3,)), dma((3, 2)), dma((3, 2)),
            dma((1,)), dma((1,)),
            dma((2, 2, 2)), dma((2, 4)),
        ],
        compiler_params=pltpu.CompilerParams(
            collective_id=0, has_side_effects=True, vmem_limit_bytes=60 * 1024 * 1024
        ),
    )(out_grad, inputs, weights)

    def back(block):
        return block.reshape(slab_len, chans, plane_size).transpose(1, 0, 2)

    return back(conv), back(grad)


def solution(mesh):
    act = P(("batch", "chan"), "slab", None)
    return jax.shard_map(
        per_device,
        mesh=mesh,
        in_specs=(act, P(None, "chan", None), act),
        out_specs=(act, act),
        check_vma=False,
    )
```

```python
import jax
import jax.numpy as jnp
from jax import lax
from jax.experimental import pallas as pl
from jax.experimental.pallas import tpu as pltpu
from jax.sharding import PartitionSpec as P

BF = jnp.bfloat16
F32 = jnp.float32
MESH = pl.DeviceIdType.MESH
NXC = 4
NYC = 4
NZC = 8


def remote(src, dst, send, recv, chan, slab, batch=None):
    where = {"chan": chan, "slab": slab}
    if batch is not None:
        where["batch"] = batch
    return pltpu.make_async_remote_copy(
        src_ref=src,
        dst_ref=dst,
        send_sem=send,
        recv_sem=recv,
        device_id=where,
        device_id_type=MESH,
    )


def arrived(ref, sem):
    pltpu.make_async_copy(ref, ref, sem).wait()


def iota(shape, dim):
    return lax.broadcasted_iota(jnp.int32, shape, dim)


def kernel(
    g_hbm, x_hbm, w_hbm, go_ref, co_ref,
    raw, tall, w_ref, in_sem,
    perm, permw, part, acts, wl, wpack, wrecv, wfwd, wbwd, outs, outr, hprod,
    loc_sem, xs, xr, zs, zr, ss, sr, ws, wr, fs, fr, yfs, yfr,
    bs, br, ybs, ybr, bx, by, os_, or_,
):
    fetch = [
        pltpu.make_async_copy(src, dst, in_sem.at[i])
        for i, (src, dst) in enumerate(
            ((g_hbm, raw.at[0]), (x_hbm, raw.at[1]), (w_hbm, w_ref))
        )
    ]
    for copy in fetch:
        copy.start()
    chan = lax.axis_index("chan")
    s = lax.axis_index("slab")
    z = chan // NXC
    x = chan % NXC
    y = lax.axis_index("batch")
    sib = 1 - s
    par = lax.rem(y, 2)
    y_next = (lax.rem(y + 1, NYC), lax.rem(y + NYC - 1, NYC))

    def at(zz, xx):
        return lax.rem(zz + 2 * NZC, NZC) * NXC + lax.rem(xx + 2 * NXC, NXC)

    barrier = pltpu.get_barrier_semaphore()
    peers = [(at(z, x), sib)]
    for k in range(1, NXC):
        peers += [(at(z, x + k), s), (at(z, x + k), sib)]
    for k in range(1, NZC):
        peers.append((at(z + k, x), s))
    for c, d in peers:
        pl.semaphore_signal(
            barrier, inc=1, device_id={"chan": c, "slab": d}, device_id_type=MESH
        )
    for b in y_next:
        pl.semaphore_signal(
            barrier, inc=1, device_id={"chan": chan, "slab": s, "batch": b},
            device_id_type=MESH,
        )

    n = iota((1, 512), 1)
    quarter, yy, zz = n // 128, (n % 128) // 16, n % 16
    main_src = yy * 64 + quarter * 16 + zz
    halo_src = yy * 64 + (quarter * 16 + jnp.where(zz < 8, -1, 16) + 64) % 64
    m = iota((512, 512), 0)
    perm[:, 0:512] = (m == main_src).astype(F32).astype(BF)
    perm[:, 512:1024] = (m == halo_src).astype(F32).astype(BF)

    lane = iota((16, 128), 1)
    halo = [jnp.zeros((16, 128), F32) for _ in range(NXC)]
    for t in range(2):
        fetch[t].wait()
        for i in range(16):
            for v in range(4):
                tall[4 * t + v, 4 * i : 4 * i + 4] = raw[
                    t, i, :, 128 * v : 128 * v + 128
                ].astype(F32)
        planes = [
            jnp.concatenate(
                [tall[4 * t + v, pl.ds(p, 16, stride=4)] for v in range(4)], axis=1
            )
            for p in range(4)
        ]
        moved = jnp.dot(
            jnp.concatenate(planes, axis=0).astype(BF), perm[...], preferred_element_type=F32
        )
        for p in range(4):
            keep = lane % 8 == (s + t) % 2 * 4 + p
            for q in range(NXC):
                rows = moved[16 * p : 16 * p + 16]
                part[q, 5 * t + p] = rows[:, 128 * q : 128 * q + 128].astype(BF)
                halo[q] = halo[q] + jnp.where(
                    keep, rows[:, 512 + 128 * q : 640 + 128 * q], 0.0
                )
    for q in range(NXC):
        part[q, 4] = halo[q].astype(BF)

    pl.semaphore_wait(barrier, len(peers) + 2)

    my_rows = pl.ds(pl.multiple_of(chan * 16, 16), 16)
    span = (pl.ds(0, 5), pl.ds(5, 4))
    chunk = (pl.ds(0, 2), pl.ds(2, 3), pl.ds(5, 2), pl.ds(7, 2))
    waits = []
    own = pltpu.make_async_copy(part.at[x], acts.at[s, :, my_rows], loc_sem.at[0])
    own.start()
    for i in range(2):
        for k in (1, 3, 2):
            dest = lax.rem(x + k, NXC)
            copy = remote(
                part.at[dest, span[i]], acts.at[s, span[i], my_rows],
                xs.at[k - 1, i], xr.at[k - 1, i], at(z, dest), s,
            )
            copy.start()
            waits.append(copy)

    half = pl.ds(pl.multiple_of(s * 256, 128), 256)
    here = pl.ds(pl.multiple_of(s * 256 + par * 128, 128), 128)
    there = pl.ds(pl.multiple_of(s * 256 + (1 - par) * 128, 128), 128)
    offsets = (pl.ds(0, 14), pl.ds(14, 13))

    def wrow(k):
        return pl.ds(pl.multiple_of(lax.rem(x + k + NXC, NXC) * 16, 16), 16)

    fetch[2].wait()
    own_w = pltpu.make_async_copy(
        w_ref.at[:, :, half], wbwd.at[:, wrow(0), half], loc_sem.at[1]
    )
    own_w.start()
    for k in (1, 3, 2):
        copy = remote(
            w_ref.at[:, :, here], wbwd.at[:, wrow(0), here],
            bs.at[k - 1], br.at[k - 1], at(z, x + k), s,
        )
        copy.start()
        waits.append(copy)

    def w_along_y(k, h):
        ref = wbwd.at[offsets[h], wrow(-k), here]
        copy = remote(ref, ref, ybs.at[k - 1, h], ybr.at[k - 1, h], chan, s, y_next[h])
        copy.start()
        waits.append(copy)

    n = iota((1, 256), 1)
    v, j, c = n // 128, (n % 128) // 32, n % 32
    permw[...] = (iota((512, 256), 0) == j * 128 + (2 * v + s) * 32 + c).astype(F32).astype(BF)
    for o in range(28):
        for t in range(4):
            at_rows, at_lanes = pl.ds(o // 4 * 16, 16), pl.ds(o % 4 * 128, 128)
            if o < 27:
                wl[t, at_rows, at_lanes] = w_ref[o, :, 128 * t : 128 * t + 128]
            else:
                wl[t, at_rows, at_lanes] = jnp.zeros((16, 128), BF)
    for t in range(4):
        packed = jnp.dot(wl[t], permw[...], preferred_element_type=F32).astype(BF)
        for v in range(2):
            for g in range(7):
                wpack[2 * t + v, g] = packed[16 * g : 16 * g + 16, 128 * v : 128 * v + 128]
    zmine = lax.rem(z, 2) == par

    def own_forward():
        return pltpu.make_async_copy(
            wpack.at[z], wrecv.at[:, z // 2, par, x], loc_sem.at[2]
        )

    def to_z(k):
        dest = lax.rem(z + k, NZC)
        return remote(
            wpack.at[dest], wrecv.at[:, z // 2, par, x], ws.at[k - 1], wr.at[k - 1],
            at(dest, x), s,
        )

    @pl.when(zmine)
    def _():
        own_forward().start()
        for k in (4, 3, 5, 2, 6, 1, 7):
            to_z(k).start()

    pairs = (pl.ds(0, 2), pl.ds(2, 2))

    def f_along_y(k, h):
        ref = wrecv.at[:, pairs[h], par, lax.rem(x - k + NXC, NXC)]
        copy = remote(ref, ref, yfs.at[k, h], yfr.at[k, h], chan, s, y_next[h])
        copy.start()
        waits.append(copy)

    def block(k):
        return pl.ds(pl.multiple_of(lax.rem(z + k + NZC, NZC) * 64, 64), 64)

    def pass_on(k, c, direction, hop):
        ref = acts.at[s, chunk[c], block(k)]
        copy = remote(
            ref, ref, zs.at[direction, hop, c], zr.at[direction, hop, c],
            at(z + (1 if direction == 0 else -1), x), s,
        )
        copy.start()
        waits.append(copy)

    def to_sibling(k, i):
        ref = acts.at[s, span[i], block(k)]
        copy = remote(
            ref, ref, ss.at[(k + NZC) % NZC, i], sr.at[(k + NZC) % NZC, i], at(z, x), sib
        )
        copy.start()
        waits.append(copy)

    own.wait()
    for i in range(2):
        for k in (1, 3, 2):
            source = lax.rem(x - k + NXC, NXC)
            rows = pl.ds(pl.multiple_of((z * NXC + source) * 16, 16), 16)
            arrived(acts.at[s, span[i], rows], xr.at[k - 1, i])
        for c in (2 * i, 2 * i + 1):
            pass_on(0, c, 0, 0)
            pass_on(0, c, 1, 0)
        to_sibling(0, i)

    def hop(h):
        for c in range(4):
            for direction in range(2):
                if h == 4 and c % 2 != direction:
                    continue
                k = -h if direction == 0 else h
                arrived(acts.at[s, chunk[c], block(k)], zr.at[direction, h - 1, c])
                if h < 3 or (h == 3 and c % 2 == direction):
                    pass_on(k, c, direction, h)
                if c % 2:
                    to_sibling(4 if h == 4 else k, c // 2)

    theirs = pl.ds(pl.multiple_of(sib * 32, 32), 32)
    mine = pl.ds(pl.multiple_of(s * 32, 32), 32)

    def back_x():
        own_w.wait()
        for k in (1, 3, 2):
            arrived(wbwd.at[:, wrow(-k), here], br.at[k - 1])
            for h in range(2):
                w_along_y(k, h)

    def forward_z():
        @pl.when(zmine)
        def _():
            own_forward().wait()

        for k in range(1, NZC):
            source = lax.rem(z - k + NZC, NZC)

            @pl.when(lax.rem(source, 2) == par)
            def _():
                arrived(wrecv.at[:, source // 2, par, x], wr.at[k - 1])

        for k in (1, 3, 2):
            ref = wrecv.at[:, :, par, x]
            copy = remote(ref, ref, fs.at[k - 1], fr.at[k - 1], at(z, x + k), s)
            copy.start()
            waits.append(copy)
        for h in range(2):
            f_along_y(0, h)

    def forward_x():
        for k in (1, 3, 2):
            arrived(wrecv.at[:, :, par, lax.rem(x - k + NXC, NXC)], fr.at[k - 1])
            for h in range(2):
                f_along_y(k, h)

    def back_y():
        for h in range(2):
            for k in (1, 3, 2):
                arrived(wbwd.at[offsets[h], wrow(-k), there], ybr.at[k - 1, h])
        swap = remote(
            wbwd.at[:, theirs, half], wbwd.at[:, theirs, half], bx.at[0], by.at[0], at(z, x), sib
        )
        swap.start()
        waits.append(swap)

    back_x()
    hop(1)
    forward_z()
    hop(2)
    forward_x()
    hop(3)
    back_y()
    hop(4)

    other = pl.ds(pl.multiple_of(sib * 256, 128), 256)
    arrived(wbwd.at[:, mine, other], by.at[0])

    def from_sibling(i):
        for k in range(NZC):
            arrived(acts.at[sib, span[i], block(k)], sr.at[k, i])

    from_sibling(0)

    lane_z = iota((32, 128), 1) % 16
    lane_k = iota((512, 128), 1) % 8

    def send_out(t, to):
        for j in range(2):
            owner = 2 * s + j
            src = outs.at[t, j, pl.ds(4 * to, 4)]
            dst = outr.at[t, x]
            itself = jnp.logical_and(owner == x, s == to)

            @pl.when(itself)
            def _():
                pltpu.make_async_copy(src, dst, or_.at[t, x]).start()

            @pl.when(jnp.logical_not(itself))
            def _():
                remote(
                    src, dst, os_.at[t, j, to], or_.at[t, x], at(z, owner), to
                ).start()

    def conv_of(weights_of, t):
        sign = 1 if t == 0 else -1
        first, second = (0, 1) if t == 0 else (1, 0)
        edge = jnp.where(lane_k < 4, acts[first, 4], acts[second, 4])
        for ai in range(3):
            hprod[3 * t + ai] = jnp.dot(weights_of(ai), edge, preferred_element_type=F32)

        def over_y(read, ci):
            total = read(3 + ci)
            for bi in (0, 2):
                shift = (16 * (bi - 1) * sign) % 128
                total = total + pltpu.roll(read(3 * bi + ci), shift, 1)
            return total

        edges = {}
        for ai in range(3):
            for ci in (0, 2):
                edges[ai, ci] = over_y(lambda r: hprod[3 * t + ai, 32 * r : 32 * r + 32], ci)
        def planes_of(to):
            for pair in (2 * to, 2 * to + 1):
                total = None
                for ai in range(3):
                    planes = [(2 * pair + i - sign * (ai - 1)) % 8 for i in range(2)]
                    both = jnp.concatenate(
                        [acts[p // 4, 5 * t + p % 4] for p in planes], axis=1
                    )
                    term = jnp.dot(weights_of(ai), both, preferred_element_type=F32)
                    total = term if total is None else total + term
                for i in range(2):
                    plane = 2 * pair + i
                    cells = total[:, 128 * i : 128 * i + 128]

                    def read(r):
                        return cells[32 * r : 32 * r + 32]

                    result = over_y(read, 1)
                    for ci in (0, 2):
                        e = sign * (ci - 1)
                        moved = pltpu.roll(over_y(read, ci), e % 128, 1)
                        outside = None
                        for ai in range(3):
                            source = (plane - sign * (ai - 1) + 4 * t) % 8
                            shift = (-source if e == 1 else 7 - source) % 128
                            term = edges[ai, ci]
                            if shift:
                                term = pltpu.roll(term, shift, 1)
                            outside = term if outside is None else outside + term
                        border = lane_z == (0 if e == 1 else 15)
                        result = result + jnp.where(border, outside, moved)
                    result = result.astype(BF)
                    for j in range(2):
                        outs[t, j, plane] = result[16 * j : 16 * j + 16]
            send_out(t, to)

        return planes_of

    def bwd_rows(ai):
        return wbwd[9 * ai : 9 * ai + 9, mine, :].reshape(288, 512)

    back = conv_of(bwd_rows, 0)
    back(1)

    from_sibling(1)

    for h in range(2):
        for k in (0, 1, 3, 2):
            column = lax.rem(x - k + NXC, NXC)
            arrived(wrecv.at[:, pairs[h], 1 - par, column], yfr.at[k, h])
    for g in range(7):
        wfwd[128 * g : 128 * g + 128, :] = wrecv[g].reshape(512, 128).T

    forth = conv_of(lambda ai: wfwd[288 * ai : 288 * ai + 288, :], 1)
    forth(1)
    back(0)
    forth(0)

    for t, ref in ((0, go_ref), (1, co_ref)):
        for q in range(NXC):
            arrived(outr.at[t, q], or_.at[t, q])
        joined = jnp.concatenate(
            [outr[t, q].reshape(64, 128) for q in range(NXC)], axis=1
        )
        ref[...] = lax.dot_general(
            joined, perm[:, 0:512], (((1,), (1,)), ((), ())), preferred_element_type=F32
        ).astype(BF)

    for copy in waits:
        copy.wait_send()

    @pl.when(zmine)
    def _():
        for k in range(1, NZC):
            to_z(k).wait_send()

    for t in range(2):
        for j in range(2):
            for to in range(2):
                owner = 2 * s + j

                @pl.when(jnp.logical_not(jnp.logical_and(owner == x, s == to)))
                def _():
                    remote(
                        outs.at[t, j, pl.ds(4 * to, 4)], outr.at[t, x],
                        os_.at[t, j, to], or_.at[t, x], at(z, owner), to,
                    ).wait_send()


def per_device(inputs, weights, out_grad):
    chans, slab_len, plane_size = inputs.shape

    vmem = pl.BlockSpec(memory_space=pltpu.VMEM)
    shape = jax.ShapeDtypeStruct((slab_len * chans, plane_size), BF)
    dma = pltpu.SemaphoreType.DMA
    grad, conv = pl.pallas_call(
        kernel,
        out_shape=(shape, shape),
        in_specs=[pl.BlockSpec(memory_space=pl.ANY)] * 3,
        out_specs=(vmem, vmem),
        scratch_shapes=[
            pltpu.VMEM((2, 16, 4, 512), BF),
            pltpu.VMEM((8, 64, 128), F32),
            pltpu.VMEM((27, 16, 512), BF),
            dma((3,)),
            pltpu.VMEM((512, 1024), BF),
            pltpu.VMEM((512, 256), BF),
            pltpu.VMEM((4, 9, 16, 128), BF),
            pltpu.VMEM((2, 9, 512, 128), BF),
            pltpu.VMEM((4, 112, 512), BF),
            pltpu.VMEM((8, 7, 16, 128), BF),
            pltpu.VMEM((7, 4, 2, 4, 16, 128), BF),
            pltpu.VMEM((896, 512), BF),
            pltpu.VMEM((27, 64, 512), BF),
            pltpu.VMEM((2, 2, 8, 16, 128), BF),
            pltpu.VMEM((2, 4, 4, 16, 128), BF),
            pltpu.VMEM((6, 288, 128), F32),
            dma((3,)),
            dma((3, 2)), dma((3, 2)),
            dma((2, 4, 4)), dma((2, 4, 4)),
            dma((8, 2)), dma((8, 2)),
            dma((7,)), dma((7,)),
            dma((3,)), dma((3,)), dma((4, 2)), dma((4, 2)),
            dma((3,)), dma((3,)), dma((3, 2)), dma((3, 2)),
            dma((1,)), dma((1,)),
            dma((2, 2, 2)), dma((2, 4)),
        ],
        compiler_params=pltpu.CompilerParams(
            collective_id=0, has_side_effects=True, vmem_limit_bytes=55104 * 1024
        ),
    )(out_grad, inputs, weights)

    def back(block):
        return block.reshape(slab_len, chans, plane_size).transpose(1, 0, 2)

    return back(conv), back(grad)


def solution(mesh):
    act = P(("batch", "chan"), "slab", None)
    return jax.shard_map(
        per_device,
        mesh=mesh,
        in_specs=(act, P(None, "chan", None), act),
        out_specs=(act, act),
        check_vma=False,
    )
```

```python
import jax
import jax.numpy as jnp
from jax import lax
from jax.experimental import pallas as pl
from jax.experimental.pallas import tpu as pltpu
from jax.sharding import PartitionSpec as P

BF = jnp.bfloat16
F32 = jnp.float32
MESH = pl.DeviceIdType.MESH
NXC = 4
NYC = 4
NZC = 8


def remote(src, dst, send, recv, chan, slab, batch=None):
    where = {"chan": chan, "slab": slab}
    if batch is not None:
        where["batch"] = batch
    return pltpu.make_async_remote_copy(
        src_ref=src,
        dst_ref=dst,
        send_sem=send,
        recv_sem=recv,
        device_id=where,
        device_id_type=MESH,
    )


def arrived(ref, sem):
    pltpu.make_async_copy(ref, ref, sem).wait()


def iota(shape, dim):
    return lax.broadcasted_iota(jnp.int32, shape, dim)


def kernel(
    g_hbm, x_hbm, w_hbm, go_ref, co_ref,
    raw, tall, w_ref, in_sem,
    perm, permw, part, acts, wl, wpack, wrecv, wfwd, wbwd, outs, outr, hprod,
    loc_sem, xs, xr, zs, zr, ss, sr, ws, wr, fs, fr, yfs, yfr,
    bs, br, ybs, ybr, bx, by, os_, or_,
):
    fetch = [
        pltpu.make_async_copy(src, dst, in_sem.at[i])
        for i, (src, dst) in enumerate(
            ((g_hbm, raw.at[0]), (x_hbm, raw.at[1]), (w_hbm, w_ref))
        )
    ]
    for copy in fetch:
        copy.start()
    chan = lax.axis_index("chan")
    s = lax.axis_index("slab")
    z = chan // NXC
    x = chan % NXC
    y = lax.axis_index("batch")
    sib = 1 - s
    par = lax.rem(y, 2)
    y_next = (lax.rem(y + 1, NYC), lax.rem(y + NYC - 1, NYC))

    def at(zz, xx):
        return lax.rem(zz + 2 * NZC, NZC) * NXC + lax.rem(xx + 2 * NXC, NXC)

    barrier = pltpu.get_barrier_semaphore()
    peers = [(at(z, x), sib)]
    for k in range(1, NXC):
        peers += [(at(z, x + k), s), (at(z, x + k), sib)]
    for k in range(1, NZC):
        peers.append((at(z + k, x), s))
    for c, d in peers:
        pl.semaphore_signal(
            barrier, inc=1, device_id={"chan": c, "slab": d}, device_id_type=MESH
        )
    for b in y_next:
        pl.semaphore_signal(
            barrier, inc=1, device_id={"chan": chan, "slab": s, "batch": b},
            device_id_type=MESH,
        )

    n = iota((1, 512), 1)
    quarter, yy, zz = n // 128, (n % 128) // 16, n % 16
    main_src = yy * 64 + quarter * 16 + zz
    halo_src = yy * 64 + (quarter * 16 + jnp.where(zz < 8, -1, 16) + 64) % 64
    m = iota((512, 512), 0)
    perm[:, 0:512] = (m == main_src).astype(F32).astype(BF)
    perm[:, 512:1024] = (m == halo_src).astype(F32).astype(BF)

    lane = iota((16, 128), 1)
    halo = [jnp.zeros((16, 128), F32) for _ in range(NXC)]
    for t in range(2):
        fetch[t].wait()
        for i in range(16):
            for v in range(4):
                tall[4 * t + v, 4 * i : 4 * i + 4] = raw[
                    t, i, :, 128 * v : 128 * v + 128
                ].astype(F32)
        planes = [
            jnp.concatenate(
                [tall[4 * t + v, pl.ds(p, 16, stride=4)] for v in range(4)], axis=1
            )
            for p in range(4)
        ]
        moved = jnp.dot(
            jnp.concatenate(planes, axis=0).astype(BF), perm[...], preferred_element_type=F32
        )
        for p in range(4):
            keep = lane % 8 == (s + t) % 2 * 4 + p
            for q in range(NXC):
                rows = moved[16 * p : 16 * p + 16]
                part[q, 5 * t + p] = rows[:, 128 * q : 128 * q + 128].astype(BF)
                halo[q] = halo[q] + jnp.where(
                    keep, rows[:, 512 + 128 * q : 640 + 128 * q], 0.0
                )
    for q in range(NXC):
        part[q, 4] = halo[q].astype(BF)

    pl.semaphore_wait(barrier, len(peers) + 2)

    my_rows = pl.ds(pl.multiple_of(chan * 16, 16), 16)
    span = (pl.ds(0, 5), pl.ds(5, 4))
    chunk = (pl.ds(0, 3), pl.ds(3, 2), pl.ds(5, 2), pl.ds(7, 2))
    waits = []
    own = pltpu.make_async_copy(part.at[x], acts.at[s, :, my_rows], loc_sem.at[0])
    own.start()
    for i in range(2):
        for k in (1, 3, 2):
            dest = lax.rem(x + k, NXC)
            copy = remote(
                part.at[dest, span[i]], acts.at[s, span[i], my_rows],
                xs.at[k - 1, i], xr.at[k - 1, i], at(z, dest), s,
            )
            copy.start()
            waits.append(copy)

    half = pl.ds(pl.multiple_of(s * 256, 128), 256)
    here = pl.ds(pl.multiple_of(s * 256 + par * 128, 128), 128)
    there = pl.ds(pl.multiple_of(s * 256 + (1 - par) * 128, 128), 128)
    offsets = (pl.ds(0, 14), pl.ds(14, 13))

    def wrow(k):
        return pl.ds(pl.multiple_of(lax.rem(x + k + NXC, NXC) * 16, 16), 16)

    fetch[2].wait()
    own_w = pltpu.make_async_copy(
        w_ref.at[:, :, half], wbwd.at[:, wrow(0), half], loc_sem.at[1]
    )
    own_w.start()
    for k in (1, 3, 2):
        copy = remote(
            w_ref.at[:, :, here], wbwd.at[:, wrow(0), here],
            bs.at[k - 1], br.at[k - 1], at(z, x + k), s,
        )
        copy.start()
        waits.append(copy)

    def w_along_y(k, h):
        ref = wbwd.at[offsets[h], wrow(-k), here]
        copy = remote(ref, ref, ybs.at[k - 1, h], ybr.at[k - 1, h], chan, s, y_next[h])
        copy.start()
        waits.append(copy)

    n = iota((1, 256), 1)
    v, j, c = n // 128, (n % 128) // 32, n % 32
    permw[...] = (iota((512, 256), 0) == j * 128 + (2 * v + s) * 32 + c).astype(F32).astype(BF)
    for o in range(28):
        for t in range(4):
            at_rows, at_lanes = pl.ds(o // 4 * 16, 16), pl.ds(o % 4 * 128, 128)
            if o < 27:
                wl[t, at_rows, at_lanes] = w_ref[o, :, 128 * t : 128 * t + 128]
            else:
                wl[t, at_rows, at_lanes] = jnp.zeros((16, 128), BF)
    for t in range(4):
        packed = jnp.dot(wl[t], permw[...], preferred_element_type=F32).astype(BF)
        for v in range(2):
            for g in range(7):
                wpack[2 * t + v, g] = packed[16 * g : 16 * g + 16, 128 * v : 128 * v + 128]
    zmine = lax.rem(z, 2) == par

    def own_forward():
        return pltpu.make_async_copy(
            wpack.at[z], wrecv.at[:, z // 2, par, x], loc_sem.at[2]
        )

    def to_z(k):
        dest = lax.rem(z + k, NZC)
        return remote(
            wpack.at[dest], wrecv.at[:, z // 2, par, x], ws.at[k - 1], wr.at[k - 1],
            at(dest, x), s,
        )

    @pl.when(zmine)
    def _():
        own_forward().start()
        for k in (4, 3, 5, 2, 6, 1, 7):
            to_z(k).start()

    pairs = (pl.ds(0, 2), pl.ds(2, 2))

    def f_along_y(k, h):
        ref = wrecv.at[:, pairs[h], par, lax.rem(x - k + NXC, NXC)]
        copy = remote(ref, ref, yfs.at[k, h], yfr.at[k, h], chan, s, y_next[h])
        copy.start()
        waits.append(copy)

    def block(k):
        return pl.ds(pl.multiple_of(lax.rem(z + k + NZC, NZC) * 64, 64), 64)

    def pass_on(k, c, direction, hop):
        ref = acts.at[s, chunk[c], block(k)]
        copy = remote(
            ref, ref, zs.at[direction, hop, c], zr.at[direction, hop, c],
            at(z + (1 if direction == 0 else -1), x), s,
        )
        copy.start()
        waits.append(copy)

    def to_sibling(k, i):
        ref = acts.at[s, span[i], block(k)]
        copy = remote(
            ref, ref, ss.at[(k + NZC) % NZC, i], sr.at[(k + NZC) % NZC, i], at(z, x), sib
        )
        copy.start()
        waits.append(copy)

    own.wait()
    for i in range(2):
        for k in (1, 3, 2):
            source = lax.rem(x - k + NXC, NXC)
            rows = pl.ds(pl.multiple_of((z * NXC + source) * 16, 16), 16)
            arrived(acts.at[s, span[i], rows], xr.at[k - 1, i])
        for c in (2 * i, 2 * i + 1):
            pass_on(0, c, 0, 0)
            pass_on(0, c, 1, 0)
        to_sibling(0, i)

    def hop(h):
        for c in range(4):
            for direction in range(2):
                if h == 4 and c % 2 != direction:
                    continue
                k = -h if direction == 0 else h
                arrived(acts.at[s, chunk[c], block(k)], zr.at[direction, h - 1, c])
                if h < 3 or (h == 3 and c % 2 == direction):
                    pass_on(k, c, direction, h)
                if c % 2:
                    to_sibling(4 if h == 4 else k, c // 2)

    theirs = pl.ds(pl.multiple_of(sib * 32, 32), 32)
    mine = pl.ds(pl.multiple_of(s * 32, 32), 32)

    def back_x():
        own_w.wait()
        for k in (1, 3, 2):
            arrived(wbwd.at[:, wrow(-k), here], br.at[k - 1])
            for h in range(2):
                w_along_y(k, h)

    def forward_z():
        @pl.when(zmine)
        def _():
            own_forward().wait()

        for k in range(1, NZC):
            source = lax.rem(z - k + NZC, NZC)

            @pl.when(lax.rem(source, 2) == par)
            def _():
                arrived(wrecv.at[:, source // 2, par, x], wr.at[k - 1])

        for k in (1, 3, 2):
            ref = wrecv.at[:, :, par, x]
            copy = remote(ref, ref, fs.at[k - 1], fr.at[k - 1], at(z, x + k), s)
            copy.start()
            waits.append(copy)
        for h in range(2):
            f_along_y(0, h)

    def forward_x():
        for k in (1, 3, 2):
            arrived(wrecv.at[:, :, par, lax.rem(x - k + NXC, NXC)], fr.at[k - 1])
            for h in range(2):
                f_along_y(k, h)

    def back_y():
        for h in range(2):
            for k in (1, 3, 2):
                arrived(wbwd.at[offsets[h], wrow(-k), there], ybr.at[k - 1, h])
        swap = remote(
            wbwd.at[:, theirs, half], wbwd.at[:, theirs, half], bx.at[0], by.at[0], at(z, x), sib
        )
        swap.start()
        waits.append(swap)

    back_x()
    hop(1)
    forward_z()
    hop(2)
    forward_x()
    back_y()
    hop(3)
    hop(4)

    other = pl.ds(pl.multiple_of(sib * 256, 128), 256)
    arrived(wbwd.at[:, mine, other], by.at[0])

    def from_sibling(i):
        for k in range(NZC):
            arrived(acts.at[sib, span[i], block(k)], sr.at[k, i])

    from_sibling(0)

    lane_z = iota((32, 128), 1) % 16
    lane_k = iota((512, 128), 1) % 8

    def send_out(t, to):
        for j in range(2):
            owner = 2 * s + j
            src = outs.at[t, j, pl.ds(4 * to, 4)]
            dst = outr.at[t, x]
            itself = jnp.logical_and(owner == x, s == to)

            @pl.when(itself)
            def _():
                pltpu.make_async_copy(src, dst, or_.at[t, x]).start()

            @pl.when(jnp.logical_not(itself))
            def _():
                remote(
                    src, dst, os_.at[t, j, to], or_.at[t, x], at(z, owner), to
                ).start()

    def conv_of(weights_of, t):
        sign = 1 if t == 0 else -1
        first, second = (0, 1) if t == 0 else (1, 0)
        edge = jnp.where(lane_k < 4, acts[first, 4], acts[second, 4])
        for ai in range(3):
            hprod[3 * t + ai] = jnp.dot(weights_of(ai), edge, preferred_element_type=F32)

        def over_y(read, ci):
            total = read(3 + ci)
            for bi in (0, 2):
                shift = (16 * (bi - 1) * sign) % 128
                total = total + pltpu.roll(read(3 * bi + ci), shift, 1)
            return total

        edges = {}
        for ai in range(3):
            for ci in (0, 2):
                edges[ai, ci] = over_y(lambda r: hprod[3 * t + ai, 32 * r : 32 * r + 32], ci)
        def planes_of(to):
            for pair in (2 * to, 2 * to + 1):
                total = None
                for ai in range(3):
                    planes = [(2 * pair + i - sign * (ai - 1)) % 8 for i in range(2)]
                    both = jnp.concatenate(
                        [acts[p // 4, 5 * t + p % 4] for p in planes], axis=1
                    )
                    term = jnp.dot(weights_of(ai), both, preferred_element_type=F32)
                    total = term if total is None else total + term
                for i in range(2):
                    plane = 2 * pair + i
                    cells = total[:, 128 * i : 128 * i + 128]

                    def read(r):
                        return cells[32 * r : 32 * r + 32]

                    result = over_y(read, 1)
                    for ci in (0, 2):
                        e = sign * (ci - 1)
                        moved = pltpu.roll(over_y(read, ci), e % 128, 1)
                        outside = None
                        for ai in range(3):
                            source = (plane - sign * (ai - 1) + 4 * t) % 8
                            shift = (-source if e == 1 else 7 - source) % 128
                            term = edges[ai, ci]
                            if shift:
                                term = pltpu.roll(term, shift, 1)
                            outside = term if outside is None else outside + term
                        border = lane_z == (0 if e == 1 else 15)
                        result = result + jnp.where(border, outside, moved)
                    result = result.astype(BF)
                    for j in range(2):
                        outs[t, j, plane] = result[16 * j : 16 * j + 16]
            send_out(t, to)

        return planes_of

    def bwd_rows(ai):
        return wbwd[9 * ai : 9 * ai + 9, mine, :].reshape(288, 512)

    back = conv_of(bwd_rows, 0)
    back(1)

    from_sibling(1)

    for h in range(2):
        for k in (0, 1, 3, 2):
            column = lax.rem(x - k + NXC, NXC)
            arrived(wrecv.at[:, pairs[h], 1 - par, column], yfr.at[k, h])
    for g in range(7):
        wfwd[128 * g : 128 * g + 128, :] = wrecv[g].reshape(512, 128).T

    forth = conv_of(lambda ai: wfwd[288 * ai : 288 * ai + 288, :], 1)
    forth(1)
    back(0)
    forth(0)

    for copy in waits:
        copy.wait_send()

    @pl.when(zmine)
    def _():
        for k in range(1, NZC):
            to_z(k).wait_send()

    for t, ref in ((0, go_ref), (1, co_ref)):
        for q in range(NXC):
            arrived(outr.at[t, q], or_.at[t, q])
        joined = jnp.concatenate(
            [outr[t, q].reshape(64, 128) for q in range(NXC)], axis=1
        )
        ref[...] = lax.dot_general(
            joined, perm[:, 0:512], (((1,), (1,)), ((), ())), preferred_element_type=F32
        ).astype(BF)

    for t in range(2):
        for j in range(2):
            for to in range(2):
                owner = 2 * s + j

                @pl.when(jnp.logical_not(jnp.logical_and(owner == x, s == to)))
                def _():
                    remote(
                        outs.at[t, j, pl.ds(4 * to, 4)], outr.at[t, x],
                        os_.at[t, j, to], or_.at[t, x], at(z, owner), to,
                    ).wait_send()


def per_device(inputs, weights, out_grad):
    chans, slab_len, plane_size = inputs.shape

    vmem = pl.BlockSpec(memory_space=pltpu.VMEM)
    shape = jax.ShapeDtypeStruct((slab_len * chans, plane_size), BF)
    dma = pltpu.SemaphoreType.DMA
    grad, conv = pl.pallas_call(
        kernel,
        out_shape=(shape, shape),
        in_specs=[pl.BlockSpec(memory_space=pl.ANY)] * 3,
        out_specs=(vmem, vmem),
        scratch_shapes=[
            pltpu.VMEM((2, 16, 4, 512), BF),
            pltpu.VMEM((8, 64, 128), F32),
            pltpu.VMEM((27, 16, 512), BF),
            dma((3,)),
            pltpu.VMEM((512, 1024), BF),
            pltpu.VMEM((512, 256), BF),
            pltpu.VMEM((4, 9, 16, 128), BF),
            pltpu.VMEM((2, 9, 512, 128), BF),
            pltpu.VMEM((4, 112, 512), BF),
            pltpu.VMEM((8, 7, 16, 128), BF),
            pltpu.VMEM((7, 4, 2, 4, 16, 128), BF),
            pltpu.VMEM((896, 512), BF),
            pltpu.VMEM((27, 64, 512), BF),
            pltpu.VMEM((2, 2, 8, 16, 128), BF),
            pltpu.VMEM((2, 4, 4, 16, 128), BF),
            pltpu.VMEM((6, 288, 128), F32),
            dma((3,)),
            dma((3, 2)), dma((3, 2)),
            dma((2, 4, 4)), dma((2, 4, 4)),
            dma((8, 2)), dma((8, 2)),
            dma((7,)), dma((7,)),
            dma((3,)), dma((3,)), dma((4, 2)), dma((4, 2)),
            dma((3,)), dma((3,)), dma((3, 2)), dma((3, 2)),
            dma((1,)), dma((1,)),
            dma((2, 2, 2)), dma((2, 4)),
        ],
        compiler_params=pltpu.CompilerParams(
            collective_id=0, has_side_effects=True, vmem_limit_bytes=55104 * 1024
        ),
    )(out_grad, inputs, weights)

    def back(block):
        return block.reshape(slab_len, chans, plane_size).transpose(1, 0, 2)

    return back(conv), back(grad)


def solution(mesh):
    act = P(("batch", "chan"), "slab", None)
    return jax.shard_map(
        per_device,
        mesh=mesh,
        in_specs=(act, P(None, "chan", None), act),
        out_specs=(act, act),
        check_vma=False,
    )
```

```python
import jax
import jax.numpy as jnp
from jax import lax
from jax.experimental import pallas as pl
from jax.experimental.pallas import tpu as pltpu
from jax.sharding import PartitionSpec as P

BF = jnp.bfloat16
F32 = jnp.float32
MESH = pl.DeviceIdType.MESH
NXC = 4
NYC = 4
NZC = 8


def remote(src, dst, send, recv, chan, slab, batch=None):
    where = {"chan": chan, "slab": slab}
    if batch is not None:
        where["batch"] = batch
    return pltpu.make_async_remote_copy(
        src_ref=src,
        dst_ref=dst,
        send_sem=send,
        recv_sem=recv,
        device_id=where,
        device_id_type=MESH,
    )


def arrived(ref, sem):
    pltpu.make_async_copy(ref, ref, sem).wait()


def iota(shape, dim):
    return lax.broadcasted_iota(jnp.int32, shape, dim)


def kernel(
    g_hbm, x_hbm, w_hbm, go_ref, co_ref,
    raw, tall, w_ref, in_sem,
    perm, permw, part, acts, wl, wpack, wrecv, wfwd, wbwd, outs, outr, hprod,
    loc_sem, xs, xr, zs, zr, ss, sr, ws, wr, fs, fr, yfs, yfr,
    bs, br, ybs, ybr, bx, by, os_, or_,
):
    fetch = [
        pltpu.make_async_copy(src, dst, in_sem.at[i])
        for i, (src, dst) in enumerate(
            ((g_hbm, raw.at[0]), (x_hbm, raw.at[1]), (w_hbm, w_ref))
        )
    ]
    for copy in fetch:
        copy.start()
    chan = lax.axis_index("chan")
    s = lax.axis_index("slab")
    z = chan // NXC
    x = chan % NXC
    y = lax.axis_index("batch")
    sib = 1 - s
    par = lax.rem(y, 2)
    y_next = (lax.rem(y + 1, NYC), lax.rem(y + NYC - 1, NYC))

    def at(zz, xx):
        return lax.rem(zz + 2 * NZC, NZC) * NXC + lax.rem(xx + 2 * NXC, NXC)

    barrier = pltpu.get_barrier_semaphore()
    peers = [(at(z, x), sib)]
    for k in range(1, NXC):
        peers += [(at(z, x + k), s), (at(z, x + k), sib)]
    for k in range(1, NZC):
        peers.append((at(z + k, x), s))
    for c, d in peers:
        pl.semaphore_signal(
            barrier, inc=1, device_id={"chan": c, "slab": d}, device_id_type=MESH
        )
    for b in y_next:
        pl.semaphore_signal(
            barrier, inc=1, device_id={"chan": chan, "slab": s, "batch": b},
            device_id_type=MESH,
        )

    n = iota((1, 512), 1)
    quarter, yy, zz = n // 128, (n % 128) // 16, n % 16
    main_src = yy * 64 + quarter * 16 + zz
    halo_src = yy * 64 + (quarter * 16 + jnp.where(zz < 8, -1, 16) + 64) % 64
    m = iota((512, 512), 0)
    perm[:, 0:512] = (m == main_src).astype(F32).astype(BF)
    perm[:, 512:1024] = (m == halo_src).astype(F32).astype(BF)

    lane = iota((16, 128), 1)
    halo = [jnp.zeros((16, 128), F32) for _ in range(NXC)]
    for t in range(2):
        fetch[t].wait()
        for i in range(16):
            for v in range(4):
                tall[4 * t + v, 4 * i : 4 * i + 4] = raw[
                    t, i, :, 128 * v : 128 * v + 128
                ].astype(F32)
        planes = [
            jnp.concatenate(
                [tall[4 * t + v, pl.ds(p, 16, stride=4)] for v in range(4)], axis=1
            )
            for p in range(4)
        ]
        moved = jnp.dot(
            jnp.concatenate(planes, axis=0).astype(BF), perm[...], preferred_element_type=F32
        )
        for p in range(4):
            keep = lane % 8 == (s + t) % 2 * 4 + p
            for q in range(NXC):
                rows = moved[16 * p : 16 * p + 16]
                part[q, 5 * t + p] = rows[:, 128 * q : 128 * q + 128].astype(BF)
                halo[q] = halo[q] + jnp.where(
                    keep, rows[:, 512 + 128 * q : 640 + 128 * q], 0.0
                )
    for q in range(NXC):
        part[q, 4] = halo[q].astype(BF)

    pl.semaphore_wait(barrier, len(peers) + 2)

    my_rows = pl.ds(pl.multiple_of(chan * 16, 16), 16)
    span = (pl.ds(0, 5), pl.ds(5, 4))
    chunk = (pl.ds(0, 3), pl.ds(3, 2), pl.ds(5, 2), pl.ds(7, 2))
    waits = []
    own = pltpu.make_async_copy(part.at[x], acts.at[s, :, my_rows], loc_sem.at[0])
    own.start()
    for k in (2, 1, 3):
        dest = lax.rem(x + k, NXC)
        copy = remote(
            part.at[dest], acts.at[s, :, my_rows],
            xs.at[k - 1, 0], xr.at[k - 1, 0], at(z, dest), s,
        )
        copy.start()
        waits.append(copy)

    half = pl.ds(pl.multiple_of(s * 256, 128), 256)
    here = pl.ds(pl.multiple_of(s * 256 + par * 128, 128), 128)
    there = pl.ds(pl.multiple_of(s * 256 + (1 - par) * 128, 128), 128)
    offsets = (pl.ds(0, 14), pl.ds(14, 13))

    def wrow(k):
        return pl.ds(pl.multiple_of(lax.rem(x + k + NXC, NXC) * 16, 16), 16)

    fetch[2].wait()
    own_w = pltpu.make_async_copy(
        w_ref.at[:, :, half], wbwd.at[:, wrow(0), half], loc_sem.at[1]
    )
    own_w.start()
    for k in (1, 3, 2):
        copy = remote(
            w_ref.at[:, :, here], wbwd.at[:, wrow(0), here],
            bs.at[k - 1], br.at[k - 1], at(z, x + k), s,
        )
        copy.start()
        waits.append(copy)

    def w_along_y(k, h):
        ref = wbwd.at[offsets[h], wrow(-k), here]
        copy = remote(ref, ref, ybs.at[k - 1, h], ybr.at[k - 1, h], chan, s, y_next[h])
        copy.start()
        waits.append(copy)

    n = iota((1, 256), 1)
    v, j, c = n // 128, (n % 128) // 32, n % 32
    permw[...] = (iota((512, 256), 0) == j * 128 + (2 * v + s) * 32 + c).astype(F32).astype(BF)
    for o in range(28):
        for t in range(4):
            at_rows, at_lanes = pl.ds(o // 4 * 16, 16), pl.ds(o % 4 * 128, 128)
            if o < 27:
                wl[t, at_rows, at_lanes] = w_ref[o, :, 128 * t : 128 * t + 128]
            else:
                wl[t, at_rows, at_lanes] = jnp.zeros((16, 128), BF)
    for t in range(4):
        packed = jnp.dot(wl[t], permw[...], preferred_element_type=F32).astype(BF)
        for v in range(2):
            for g in range(7):
                wpack[2 * t + v, g] = packed[16 * g : 16 * g + 16, 128 * v : 128 * v + 128]
    zmine = lax.rem(z, 2) == par

    def own_forward():
        return pltpu.make_async_copy(
            wpack.at[z], wrecv.at[:, z // 2, par, x], loc_sem.at[2]
        )

    def to_z(k):
        dest = lax.rem(z + k, NZC)
        return remote(
            wpack.at[dest], wrecv.at[:, z // 2, par, x], ws.at[k - 1], wr.at[k - 1],
            at(dest, x), s,
        )

    @pl.when(zmine)
    def _():
        own_forward().start()
        for k in (4, 3, 5, 2, 6, 1, 7):
            to_z(k).start()

    pairs = (pl.ds(0, 2), pl.ds(2, 2))

    def f_along_y(k, h):
        ref = wrecv.at[:, pairs[h], par, lax.rem(x - k + NXC, NXC)]
        copy = remote(ref, ref, yfs.at[k, h], yfr.at[k, h], chan, s, y_next[h])
        copy.start()
        waits.append(copy)

    def block(k):
        return pl.ds(pl.multiple_of(lax.rem(z + k + NZC, NZC) * 64, 64), 64)

    def pass_on(k, c, direction, hop):
        ref = acts.at[s, chunk[c], block(k)]
        copy = remote(
            ref, ref, zs.at[direction, hop, c], zr.at[direction, hop, c],
            at(z + (1 if direction == 0 else -1), x), s,
        )
        copy.start()
        waits.append(copy)

    def to_sibling(k, i):
        ref = acts.at[s, span[i], block(k)]
        copy = remote(
            ref, ref, ss.at[(k + NZC) % NZC, i], sr.at[(k + NZC) % NZC, i], at(z, x), sib
        )
        copy.start()
        waits.append(copy)

    own.wait()
    for k in (1, 3, 2):
        rows = pl.ds(pl.multiple_of(at(z, x - k) * 16, 16), 16)
        arrived(acts.at[s, :, rows], xr.at[k - 1, 0])
    for i in range(2):
        for c in (2 * i, 2 * i + 1):
            pass_on(0, c, 0, 0)
            pass_on(0, c, 1, 0)
        to_sibling(0, i)

    def hop(h):
        for c in range(4):
            for direction in range(2):
                if h == 4 and c % 2 != direction:
                    continue
                k = -h if direction == 0 else h
                arrived(acts.at[s, chunk[c], block(k)], zr.at[direction, h - 1, c])
                if h < 3 or (h == 3 and c % 2 == direction):
                    pass_on(k, c, direction, h)
                if c % 2:
                    to_sibling(4 if h == 4 else k, c // 2)

    theirs = pl.ds(pl.multiple_of(sib * 32, 32), 32)
    mine = pl.ds(pl.multiple_of(s * 32, 32), 32)

    def back_x():
        own_w.wait()
        for k in (1, 3, 2):
            arrived(wbwd.at[:, wrow(-k), here], br.at[k - 1])
            for h in range(2):
                w_along_y(k, h)

    def forward_z():
        @pl.when(zmine)
        def _():
            own_forward().wait()

        for k in range(1, NZC):
            source = lax.rem(z - k + NZC, NZC)

            @pl.when(lax.rem(source, 2) == par)
            def _():
                arrived(wrecv.at[:, source // 2, par, x], wr.at[k - 1])

        for k in (1, 3, 2):
            ref = wrecv.at[:, :, par, x]
            copy = remote(ref, ref, fs.at[k - 1], fr.at[k - 1], at(z, x + k), s)
            copy.start()
            waits.append(copy)
        for h in range(2):
            f_along_y(0, h)

    def forward_x():
        for k in (1, 3, 2):
            arrived(wrecv.at[:, :, par, lax.rem(x - k + NXC, NXC)], fr.at[k - 1])
            for h in range(2):
                f_along_y(k, h)

    def back_y():
        for h in range(2):
            for k in (1, 3, 2):
                arrived(wbwd.at[offsets[h], wrow(-k), there], ybr.at[k - 1, h])
        swap = remote(
            wbwd.at[:, theirs, half], wbwd.at[:, theirs, half], bx.at[0], by.at[0], at(z, x), sib
        )
        swap.start()
        waits.append(swap)

    back_x()
    hop(1)
    forward_z()
    hop(2)
    forward_x()
    back_y()
    hop(3)
    hop(4)

    other = pl.ds(pl.multiple_of(sib * 256, 128), 256)
    arrived(wbwd.at[:, mine, other], by.at[0])

    def from_sibling(i):
        for k in range(NZC):
            arrived(acts.at[sib, span[i], block(k)], sr.at[k, i])

    from_sibling(0)

    lane_z = iota((32, 128), 1) % 16
    lane_k = iota((512, 128), 1) % 8

    def send_out(t, to):
        for j in range(2):
            owner = 2 * s + j
            src = outs.at[t, j, pl.ds(4 * to, 4)]
            dst = outr.at[t, x]
            itself = jnp.logical_and(owner == x, s == to)

            @pl.when(itself)
            def _():
                pltpu.make_async_copy(src, dst, or_.at[t, x]).start()

            @pl.when(jnp.logical_not(itself))
            def _():
                remote(
                    src, dst, os_.at[t, j, to], or_.at[t, x], at(z, owner), to
                ).start()

    def conv_of(weights_of, t):
        sign = 1 if t == 0 else -1
        first, second = (0, 1) if t == 0 else (1, 0)
        edge = jnp.where(lane_k < 4, acts[first, 4], acts[second, 4])
        for ai in range(3):
            hprod[3 * t + ai] = jnp.dot(weights_of(ai), edge, preferred_element_type=F32)

        def over_y(read, ci):
            total = read(3 + ci)
            for bi in (0, 2):
                shift = (16 * (bi - 1) * sign) % 128
                total = total + pltpu.roll(read(3 * bi + ci), shift, 1)
            return total

        edges = {}
        for ai in range(3):
            for ci in (0, 2):
                edges[ai, ci] = over_y(lambda r: hprod[3 * t + ai, 32 * r : 32 * r + 32], ci)
        def planes_of(to):
            for pair in (2 * to, 2 * to + 1):
                total = None
                for ai in range(3):
                    planes = [(2 * pair + i - sign * (ai - 1)) % 8 for i in range(2)]
                    both = jnp.concatenate(
                        [acts[p // 4, 5 * t + p % 4] for p in planes], axis=1
                    )
                    term = jnp.dot(weights_of(ai), both, preferred_element_type=F32)
                    total = term if total is None else total + term
                for i in range(2):
                    plane = 2 * pair + i
                    cells = total[:, 128 * i : 128 * i + 128]

                    def read(r):
                        return cells[32 * r : 32 * r + 32]

                    result = over_y(read, 1)
                    for ci in (0, 2):
                        e = sign * (ci - 1)
                        moved = pltpu.roll(over_y(read, ci), e % 128, 1)
                        outside = None
                        for ai in range(3):
                            source = (plane - sign * (ai - 1) + 4 * t) % 8
                            shift = (-source if e == 1 else 7 - source) % 128
                            term = edges[ai, ci]
                            if shift:
                                term = pltpu.roll(term, shift, 1)
                            outside = term if outside is None else outside + term
                        border = lane_z == (0 if e == 1 else 15)
                        result = result + jnp.where(border, outside, moved)
                    result = result.astype(BF)
                    for j in range(2):
                        outs[t, j, plane] = result[16 * j : 16 * j + 16]
            send_out(t, to)

        return planes_of

    def bwd_rows(ai):
        return wbwd[9 * ai : 9 * ai + 9, mine, :].reshape(288, 512)

    back = conv_of(bwd_rows, 0)
    back(1)

    from_sibling(1)

    for h in range(2):
        for k in (0, 1, 3, 2):
            column = lax.rem(x - k + NXC, NXC)
            arrived(wrecv.at[:, pairs[h], 1 - par, column], yfr.at[k, h])
    for g in range(7):
        wfwd[128 * g : 128 * g + 128, :] = wrecv[g].reshape(512, 128).T

    forth = conv_of(lambda ai: wfwd[288 * ai : 288 * ai + 288, :], 1)
    forth(1)
    back(0)
    forth(0)

    for copy in waits:
        copy.wait_send()

    @pl.when(zmine)
    def _():
        for k in range(1, NZC):
            to_z(k).wait_send()

    for t, ref in ((0, go_ref), (1, co_ref)):
        for q in range(NXC):
            arrived(outr.at[t, q], or_.at[t, q])
        joined = jnp.concatenate(
            [outr[t, q].reshape(64, 128) for q in range(NXC)], axis=1
        )
        ref[...] = lax.dot_general(
            joined, perm[:, 0:512], (((1,), (1,)), ((), ())), preferred_element_type=F32
        ).astype(BF)

    for t in range(2):
        for j in range(2):
            for to in range(2):
                owner = 2 * s + j

                @pl.when(jnp.logical_not(jnp.logical_and(owner == x, s == to)))
                def _():
                    remote(
                        outs.at[t, j, pl.ds(4 * to, 4)], outr.at[t, x],
                        os_.at[t, j, to], or_.at[t, x], at(z, owner), to,
                    ).wait_send()


def per_device(inputs, weights, out_grad):
    chans, slab_len, plane_size = inputs.shape

    vmem = pl.BlockSpec(memory_space=pltpu.VMEM)
    shape = jax.ShapeDtypeStruct((slab_len * chans, plane_size), BF)
    dma = pltpu.SemaphoreType.DMA
    grad, conv = pl.pallas_call(
        kernel,
        out_shape=(shape, shape),
        in_specs=[pl.BlockSpec(memory_space=pl.ANY)] * 3,
        out_specs=(vmem, vmem),
        scratch_shapes=[
            pltpu.VMEM((2, 16, 4, 512), BF),
            pltpu.VMEM((8, 64, 128), F32),
            pltpu.VMEM((27, 16, 512), BF),
            dma((3,)),
            pltpu.VMEM((512, 1024), BF),
            pltpu.VMEM((512, 256), BF),
            pltpu.VMEM((4, 9, 16, 128), BF),
            pltpu.VMEM((2, 9, 512, 128), BF),
            pltpu.VMEM((4, 112, 512), BF),
            pltpu.VMEM((8, 7, 16, 128), BF),
            pltpu.VMEM((7, 4, 2, 4, 16, 128), BF),
            pltpu.VMEM((896, 512), BF),
            pltpu.VMEM((27, 64, 512), BF),
            pltpu.VMEM((2, 2, 8, 16, 128), BF),
            pltpu.VMEM((2, 4, 4, 16, 128), BF),
            pltpu.VMEM((6, 288, 128), F32),
            dma((3,)),
            dma((3, 2)), dma((3, 2)),
            dma((2, 4, 4)), dma((2, 4, 4)),
            dma((8, 2)), dma((8, 2)),
            dma((7,)), dma((7,)),
            dma((3,)), dma((3,)), dma((4, 2)), dma((4, 2)),
            dma((3,)), dma((3,)), dma((3, 2)), dma((3, 2)),
            dma((1,)), dma((1,)),
            dma((2, 2, 2)), dma((2, 4)),
        ],
        compiler_params=pltpu.CompilerParams(
            collective_id=0, has_side_effects=True, vmem_limit_bytes=55104 * 1024
        ),
    )(out_grad, inputs, weights)

    def back(block):
        return block.reshape(slab_len, chans, plane_size).transpose(1, 0, 2)

    return back(conv), back(grad)


def solution(mesh):
    act = P(("batch", "chan"), "slab", None)
    return jax.shard_map(
        per_device,
        mesh=mesh,
        in_specs=(act, P(None, "chan", None), act),
        out_specs=(act, act),
        check_vma=False,
    )
```

```python
import jax
import jax.numpy as jnp
from jax import lax
from jax.experimental import pallas as pl
from jax.experimental.pallas import tpu as pltpu
from jax.sharding import PartitionSpec as P

BF = jnp.bfloat16
F32 = jnp.float32
MESH = pl.DeviceIdType.MESH
NXC = 4
NYC = 4
NZC = 8


def remote(src, dst, send, recv, chan, slab, batch=None):
    where = {"chan": chan, "slab": slab}
    if batch is not None:
        where["batch"] = batch
    return pltpu.make_async_remote_copy(
        src_ref=src,
        dst_ref=dst,
        send_sem=send,
        recv_sem=recv,
        device_id=where,
        device_id_type=MESH,
    )


def arrived(ref, sem):
    pltpu.make_async_copy(ref, ref, sem).wait()


def iota(shape, dim):
    return lax.broadcasted_iota(jnp.int32, shape, dim)


def kernel(
    g_hbm, x_hbm, w_hbm, go_ref, co_ref,
    raw, tall, w_ref, in_sem,
    perm, permw, part, acts, wl, wpack, wrecv, wfwd, wbwd, outs, outr, hprod,
    loc_sem, xs, xr, zs, zr, ss, sr, ws, wr, fs, fr, yfs, yfr,
    bs, br, ybs, ybr, bx, by, os_, or_,
):
    fetch = [
        pltpu.make_async_copy(src, dst, in_sem.at[i])
        for i, (src, dst) in enumerate(
            ((g_hbm, raw.at[0]), (x_hbm, raw.at[1]), (w_hbm, w_ref))
        )
    ]
    for copy in fetch:
        copy.start()
    chan = lax.axis_index("chan")
    s = lax.axis_index("slab")
    z = chan // NXC
    x = chan % NXC
    y = lax.axis_index("batch")
    sib = 1 - s
    par = lax.rem(y, 2)
    y_next = (lax.rem(y + 1, NYC), lax.rem(y + NYC - 1, NYC))

    def at(zz, xx):
        return lax.rem(zz + 2 * NZC, NZC) * NXC + lax.rem(xx + 2 * NXC, NXC)

    barrier = pltpu.get_barrier_semaphore()
    peers = [(at(z, x), sib)]
    for k in range(1, NXC):
        peers += [(at(z, x + k), s), (at(z, x + k), sib)]
    for k in range(1, NZC):
        peers.append((at(z + k, x), s))
    for c, d in peers:
        pl.semaphore_signal(
            barrier, inc=1, device_id={"chan": c, "slab": d}, device_id_type=MESH
        )
    for b in y_next:
        pl.semaphore_signal(
            barrier, inc=1, device_id={"chan": chan, "slab": s, "batch": b},
            device_id_type=MESH,
        )

    n = iota((1, 512), 1)
    quarter, yy, zz = n // 128, (n % 128) // 16, n % 16
    main_src = yy * 64 + quarter * 16 + zz
    halo_src = yy * 64 + (quarter * 16 + jnp.where(zz < 8, -1, 16) + 64) % 64
    m = iota((512, 512), 0)
    perm[:, 0:512] = (m == main_src).astype(F32).astype(BF)
    perm[:, 512:1024] = (m == halo_src).astype(F32).astype(BF)

    lane = iota((16, 128), 1)
    halo = [jnp.zeros((16, 128), F32) for _ in range(NXC)]
    for t in range(2):
        fetch[t].wait()
        for i in range(16):
            for v in range(4):
                tall[4 * t + v, 4 * i : 4 * i + 4] = raw[
                    t, i, :, 128 * v : 128 * v + 128
                ].astype(F32)
        planes = [
            jnp.concatenate(
                [tall[4 * t + v, pl.ds(p, 16, stride=4)] for v in range(4)], axis=1
            )
            for p in range(4)
        ]
        moved = jnp.dot(
            jnp.concatenate(planes, axis=0).astype(BF), perm[...], preferred_element_type=F32
        )
        for p in range(4):
            keep = lane % 8 == (s + t) % 2 * 4 + p
            for q in range(NXC):
                rows = moved[16 * p : 16 * p + 16]
                part[q, 5 * t + p] = rows[:, 128 * q : 128 * q + 128].astype(BF)
                halo[q] = halo[q] + jnp.where(
                    keep, rows[:, 512 + 128 * q : 640 + 128 * q], 0.0
                )
    for q in range(NXC):
        part[q, 4] = halo[q].astype(BF)

    pl.semaphore_wait(barrier, len(peers) + 2)

    my_rows = pl.ds(pl.multiple_of(chan * 16, 16), 16)
    span = (pl.ds(0, 5), pl.ds(5, 4))
    chunk = (pl.ds(0, 3), pl.ds(3, 2), pl.ds(5, 2), pl.ds(7, 2))
    waits = []
    own = pltpu.make_async_copy(part.at[x], acts.at[s, :, my_rows], loc_sem.at[0])
    own.start()
    for k in (2, 1, 3):
        dest = lax.rem(x + k, NXC)
        copy = remote(
            part.at[dest], acts.at[s, :, my_rows],
            xs.at[k - 1, 0], xr.at[k - 1, 0], at(z, dest), s,
        )
        copy.start()
        waits.append(copy)

    half = pl.ds(pl.multiple_of(s * 256, 128), 256)
    here = pl.ds(pl.multiple_of(s * 256 + par * 128, 128), 128)
    there = pl.ds(pl.multiple_of(s * 256 + (1 - par) * 128, 128), 128)
    offsets = (pl.ds(0, 14), pl.ds(14, 13))

    def wrow(k):
        return pl.ds(pl.multiple_of(lax.rem(x + k + NXC, NXC) * 16, 16), 16)

    fetch[2].wait()
    own_w = pltpu.make_async_copy(
        w_ref.at[:, :, half], wbwd.at[:, wrow(0), half], loc_sem.at[1]
    )
    own_w.start()
    for k in (1, 3, 2):
        copy = remote(
            w_ref.at[:, :, here], wbwd.at[:, wrow(0), here],
            bs.at[k - 1], br.at[k - 1], at(z, x + k), s,
        )
        copy.start()
        waits.append(copy)

    def w_along_y(k, h):
        ref = wbwd.at[offsets[h], wrow(-k), here]
        copy = remote(ref, ref, ybs.at[k - 1, h], ybr.at[k - 1, h], chan, s, y_next[h])
        copy.start()
        waits.append(copy)

    n = iota((1, 256), 1)
    v, j, c = n // 128, (n % 128) // 32, n % 32
    permw[...] = (iota((512, 256), 0) == j * 128 + (2 * v + s) * 32 + c).astype(F32).astype(BF)
    for o in range(28):
        for t in range(4):
            at_rows, at_lanes = pl.ds(o // 4 * 16, 16), pl.ds(o % 4 * 128, 128)
            if o < 27:
                wl[t, at_rows, at_lanes] = w_ref[o, :, 128 * t : 128 * t + 128]
            else:
                wl[t, at_rows, at_lanes] = jnp.zeros((16, 128), BF)
    for t in range(4):
        packed = jnp.dot(wl[t], permw[...], preferred_element_type=F32).astype(BF)
        for v in range(2):
            for g in range(7):
                wpack[2 * t + v, g] = packed[16 * g : 16 * g + 16, 128 * v : 128 * v + 128]
    zmine = lax.rem(z, 2) == par

    def own_forward():
        return pltpu.make_async_copy(
            wpack.at[z], wrecv.at[:, z // 2, par, x], loc_sem.at[2]
        )

    def to_z(k):
        dest = lax.rem(z + k, NZC)
        return remote(
            wpack.at[dest], wrecv.at[:, z // 2, par, x], ws.at[k - 1], wr.at[k - 1],
            at(dest, x), s,
        )

    @pl.when(zmine)
    def _():
        own_forward().start()
        for k in (4, 3, 5, 2, 6, 1, 7):
            to_z(k).start()

    pairs = (pl.ds(0, 2), pl.ds(2, 2))

    def f_along_y(k, h):
        ref = wrecv.at[:, pairs[h], par, lax.rem(x - k + NXC, NXC)]
        copy = remote(ref, ref, yfs.at[k, h], yfr.at[k, h], chan, s, y_next[h])
        copy.start()
        waits.append(copy)

    def block(k):
        return pl.ds(pl.multiple_of(lax.rem(z + k + NZC, NZC) * 64, 64), 64)

    def pass_on(k, c, direction, hop):
        ref = acts.at[s, chunk[c], block(k)]
        copy = remote(
            ref, ref, zs.at[direction, hop, c], zr.at[direction, hop, c],
            at(z + (1 if direction == 0 else -1), x), s,
        )
        copy.start()
        waits.append(copy)

    def to_sibling(k, i):
        ref = acts.at[s, span[i], block(k)]
        copy = remote(
            ref, ref, ss.at[(k + NZC) % NZC, i], sr.at[(k + NZC) % NZC, i], at(z, x), sib
        )
        copy.start()
        waits.append(copy)

    own.wait()
    for k in (1, 3, 2):
        rows = pl.ds(pl.multiple_of(at(z, x - k) * 16, 16), 16)
        arrived(acts.at[s, :, rows], xr.at[k - 1, 0])
    for i in range(2):
        for c in (2 * i, 2 * i + 1):
            pass_on(0, c, 0, 0)
            pass_on(0, c, 1, 0)
        to_sibling(0, i)

    def hop(h):
        for c in range(4):
            for direction in range(2):
                if h == 4 and c % 2 != direction:
                    continue
                k = -h if direction == 0 else h
                arrived(acts.at[s, chunk[c], block(k)], zr.at[direction, h - 1, c])
                if h < 3 or (h == 3 and c % 2 == direction):
                    pass_on(k, c, direction, h)
                if c % 2:
                    to_sibling(4 if h == 4 else k, c // 2)

    theirs = pl.ds(pl.multiple_of(sib * 32, 32), 32)
    mine = pl.ds(pl.multiple_of(s * 32, 32), 32)

    def back_x():
        own_w.wait()
        for k in (1, 3, 2):
            arrived(wbwd.at[:, wrow(-k), here], br.at[k - 1])
            for h in range(2):
                w_along_y(k, h)

    def forward_z():
        @pl.when(zmine)
        def _():
            own_forward().wait()

        for k in range(1, NZC):
            source = lax.rem(z - k + NZC, NZC)

            @pl.when(lax.rem(source, 2) == par)
            def _():
                arrived(wrecv.at[:, source // 2, par, x], wr.at[k - 1])

        for k in (1, 3, 2):
            ref = wrecv.at[:, :, par, x]
            copy = remote(ref, ref, fs.at[k - 1], fr.at[k - 1], at(z, x + k), s)
            copy.start()
            waits.append(copy)
        for h in range(2):
            f_along_y(0, h)

    def forward_x():
        for k in (1, 3, 2):
            arrived(wrecv.at[:, :, par, lax.rem(x - k + NXC, NXC)], fr.at[k - 1])
            for h in range(2):
                f_along_y(k, h)

    def back_y():
        for h in range(2):
            for k in (1, 3, 2):
                arrived(wbwd.at[offsets[h], wrow(-k), there], ybr.at[k - 1, h])
        swap = remote(
            wbwd.at[:, theirs, half], wbwd.at[:, theirs, half], bx.at[0], by.at[0], at(z, x), sib
        )
        swap.start()
        waits.append(swap)

    back_x()
    hop(1)
    forward_z()
    hop(2)
    forward_x()
    back_y()
    hop(3)
    hop(4)

    other = pl.ds(pl.multiple_of(sib * 256, 128), 256)
    arrived(wbwd.at[:, mine, other], by.at[0])

    def from_sibling(i):
        for k in range(NZC):
            arrived(acts.at[sib, span[i], block(k)], sr.at[k, i])

    for h in range(2):
        for k in (0, 1, 3, 2):
            column = lax.rem(x - k + NXC, NXC)
            arrived(wrecv.at[:, pairs[h], 1 - par, column], yfr.at[k, h])
    for g in range(7):
        wfwd[128 * g : 128 * g + 128, :] = wrecv[g].reshape(512, 128).T

    from_sibling(0)

    lane_z = iota((32, 128), 1) % 16
    lane_k = iota((512, 128), 1) % 8

    def send_out(t, to):
        for j in range(2):
            owner = 2 * s + j
            src = outs.at[t, j, pl.ds(4 * to, 4)]
            dst = outr.at[t, x]
            itself = jnp.logical_and(owner == x, s == to)

            @pl.when(itself)
            def _():
                pltpu.make_async_copy(src, dst, or_.at[t, x]).start()

            @pl.when(jnp.logical_not(itself))
            def _():
                remote(
                    src, dst, os_.at[t, j, to], or_.at[t, x], at(z, owner), to
                ).start()

    def conv_of(weights_of, t):
        sign = 1 if t == 0 else -1
        first, second = (0, 1) if t == 0 else (1, 0)
        edge = jnp.where(lane_k < 4, acts[first, 4], acts[second, 4])
        for ai in range(3):
            hprod[3 * t + ai] = jnp.dot(weights_of(ai), edge, preferred_element_type=F32)

        def over_y(read, ci):
            total = read(3 + ci)
            for bi in (0, 2):
                shift = (16 * (bi - 1) * sign) % 128
                total = total + pltpu.roll(read(3 * bi + ci), shift, 1)
            return total

        edges = {}
        for ai in range(3):
            for ci in (0, 2):
                edges[ai, ci] = over_y(lambda r: hprod[3 * t + ai, 32 * r : 32 * r + 32], ci)
        def planes_of(to):
            for pair in (2 * to, 2 * to + 1):
                total = None
                for ai in range(3):
                    planes = [(2 * pair + i - sign * (ai - 1)) % 8 for i in range(2)]
                    both = jnp.concatenate(
                        [acts[p // 4, 5 * t + p % 4] for p in planes], axis=1
                    )
                    term = jnp.dot(weights_of(ai), both, preferred_element_type=F32)
                    total = term if total is None else total + term
                for i in range(2):
                    plane = 2 * pair + i
                    cells = total[:, 128 * i : 128 * i + 128]

                    def read(r):
                        return cells[32 * r : 32 * r + 32]

                    result = over_y(read, 1)
                    for ci in (0, 2):
                        e = sign * (ci - 1)
                        moved = pltpu.roll(over_y(read, ci), e % 128, 1)
                        outside = None
                        for ai in range(3):
                            source = (plane - sign * (ai - 1) + 4 * t) % 8
                            shift = (-source if e == 1 else 7 - source) % 128
                            term = edges[ai, ci]
                            if shift:
                                term = pltpu.roll(term, shift, 1)
                            outside = term if outside is None else outside + term
                        border = lane_z == (0 if e == 1 else 15)
                        result = result + jnp.where(border, outside, moved)
                    result = result.astype(BF)
                    for j in range(2):
                        outs[t, j, plane] = result[16 * j : 16 * j + 16]
            send_out(t, to)

        return planes_of

    def bwd_rows(ai):
        return wbwd[9 * ai : 9 * ai + 9, mine, :].reshape(288, 512)

    back = conv_of(bwd_rows, 0)
    back(1)

    from_sibling(1)

    forth = conv_of(lambda ai: wfwd[288 * ai : 288 * ai + 288, :], 1)
    forth(1)
    back(0)
    forth(0)

    for copy in waits:
        copy.wait_send()

    @pl.when(zmine)
    def _():
        for k in range(1, NZC):
            to_z(k).wait_send()

    for t, ref in ((0, go_ref), (1, co_ref)):
        for q in range(NXC):
            arrived(outr.at[t, q], or_.at[t, q])
        joined = jnp.concatenate(
            [outr[t, q].reshape(64, 128) for q in range(NXC)], axis=1
        )
        ref[...] = lax.dot_general(
            joined, perm[:, 0:512], (((1,), (1,)), ((), ())), preferred_element_type=F32
        ).astype(BF)

    for t in range(2):
        for j in range(2):
            for to in range(2):
                owner = 2 * s + j

                @pl.when(jnp.logical_not(jnp.logical_and(owner == x, s == to)))
                def _():
                    remote(
                        outs.at[t, j, pl.ds(4 * to, 4)], outr.at[t, x],
                        os_.at[t, j, to], or_.at[t, x], at(z, owner), to,
                    ).wait_send()


def per_device(inputs, weights, out_grad):
    chans, slab_len, plane_size = inputs.shape

    vmem = pl.BlockSpec(memory_space=pltpu.VMEM)
    shape = jax.ShapeDtypeStruct((slab_len * chans, plane_size), BF)
    dma = pltpu.SemaphoreType.DMA
    grad, conv = pl.pallas_call(
        kernel,
        out_shape=(shape, shape),
        in_specs=[pl.BlockSpec(memory_space=pl.ANY)] * 3,
        out_specs=(vmem, vmem),
        scratch_shapes=[
            pltpu.VMEM((2, 16, 4, 512), BF),
            pltpu.VMEM((8, 64, 128), F32),
            pltpu.VMEM((27, 16, 512), BF),
            dma((3,)),
            pltpu.VMEM((512, 1024), BF),
            pltpu.VMEM((512, 256), BF),
            pltpu.VMEM((4, 9, 16, 128), BF),
            pltpu.VMEM((2, 9, 512, 128), BF),
            pltpu.VMEM((4, 112, 512), BF),
            pltpu.VMEM((8, 7, 16, 128), BF),
            pltpu.VMEM((7, 4, 2, 4, 16, 128), BF),
            pltpu.VMEM((896, 512), BF),
            pltpu.VMEM((27, 64, 512), BF),
            pltpu.VMEM((2, 2, 8, 16, 128), BF),
            pltpu.VMEM((2, 4, 4, 16, 128), BF),
            pltpu.VMEM((6, 288, 128), F32),
            dma((3,)),
            dma((3, 2)), dma((3, 2)),
            dma((2, 4, 4)), dma((2, 4, 4)),
            dma((8, 2)), dma((8, 2)),
            dma((7,)), dma((7,)),
            dma((3,)), dma((3,)), dma((4, 2)), dma((4, 2)),
            dma((3,)), dma((3,)), dma((3, 2)), dma((3, 2)),
            dma((1,)), dma((1,)),
            dma((2, 2, 2)), dma((2, 4)),
        ],
        compiler_params=pltpu.CompilerParams(
            collective_id=0, has_side_effects=True, vmem_limit_bytes=55104 * 1024
        ),
    )(out_grad, inputs, weights)

    def back(block):
        return block.reshape(slab_len, chans, plane_size).transpose(1, 0, 2)

    return back(conv), back(grad)


def solution(mesh):
    act = P(("batch", "chan"), "slab", None)
    return jax.shard_map(
        per_device,
        mesh=mesh,
        in_specs=(act, P(None, "chan", None), act),
        out_specs=(act, act),
        check_vma=False,
    )
```
